32 devices in a mesh: exp: 4 (over x, core), fsdp: 8 (over z, y).
Axes of the slice: x: 2, y: 2, z: 4, core: 2. Of those that a mesh axis runs over, the one named last changes fastest.
Arguments:
- tokens: bfloat16 [4096, 1536], P(('exp', 'fsdp')), may hold values from -6 to 6
- expert_ids: int32 [4096, 2], P(('exp', 'fsdp')), may hold values from 0 to 3, all different within a row; in each aligned block of 128 rows (0 to 127, 128 to 255, ...) at most 96 rows name the same one
- gates: float32 [4096, 2], P(('exp', 'fsdp')), may hold values from 0.1 to 1
- w_in: bfloat16 [4, 2048, 1536], P('exp', 'fsdp'), may hold values from -0.15625 to 0.15625
- w_out: bfloat16 [4, 2048, 1536], P('exp', 'fsdp'), may hold values from -0.125 to 0.125
- grad_y: bfloat16 [4096, 1536], P(('exp', 'fsdp')), may hold values from -6 to 6
Outputs:
- mixed: bfloat16 [4096, 1536], P(('exp', 'fsdp'))
- grad_tokens: bfloat16 [4096, 1536], P(('exp', 'fsdp'))
- grad_w_in: float32 [4, 2048, 1536], P('exp', 'fsdp')
- grad_w_out: float32 [4, 2048, 1536], P('exp', 'fsdp')
- grad_gates: float32 [4096, 2], P(('exp', 'fsdp'))
The draws below stay inside these ranges and needn't reach their ends.
Inputs may be any that keep to these rules, and one draw needn't show every extreme that they name: `expert_ids`: each row names two different experts. Among the rows of one device no expert is named by more than 96 rows, and in some device some expert is named by exactly 96 rows.
All inputs are finite; a program needn't handle non-finite values.
Results may differ from the reference program's by a relative error of at most 0.0065.
Values may be sent and summed in bfloat16 or wider, within the bound.
No kernel may reach another device: no remote copies, remote signals or barrier semaphores. Data moves between devices by JAX's collectives and lax.ppermute only.
A program may use at most 192 MiB of HBM per device.

```python
import math
import jax
import jax.numpy as jnp
import numpy as np
from jax import lax

D = 1536
H = 2048
TOK_DEV = 128
EXPERTS = 4
CAP = 96
TOKENS = 4096
N_EXP = 4
N_FSDP = 8


def level_of(own_key, shape, shards, low, top_value):
    def one(position, parts):
        steps = jax.random.uniform(jax.random.fold_in(jax.random.fold_in(own_key, 6), position), (parts,), jnp.float32, low / len(shards), top_value / len(shards))
        return jnp.repeat(jnp.exp(steps), shape[position] // parts).reshape((-1,) + (1,) * (len(shape) - position - 1))

    factor_of = one(*shards[0])
    for cut in shards[1:]:
        factor_of = factor_of * one(*cut)
    return factor_of


def routed_block(rng, own, number, rows, number_of, top, limit, skew):
    ranking = jax.random.permutation(rng, number_of)
    heavy_load, usual = shares(number_of, rows * top, limit, skew, True), shares(number_of, rows * top, limit, skew, False)
    places = jnp.arange(number_of)

    def named(sizes, offset_by):
        used = int((sizes > 0).sum())
        fixed = max(1, used // 4)
        moved = fixed + (places - fixed + offset_by * (used - fixed)) % max(1, number_of - fixed)
        return jnp.zeros((number_of,), jnp.int32).at[ranking[jnp.where(places < fixed, places, moved)]].set(jnp.asarray(sizes, jnp.int32))

    sizes = jnp.where(number % 4 == 0, named(heavy_load, number // 4), named(usual, number - number // 4 - 1))
    mixed = jax.random.permutation(jax.random.fold_in(own, 3), number_of)
    source_of, taker = mixed[0:number_of // 2 * 2:2], mixed[1:number_of // 2 * 2:2]
    room = jnp.minimum(sizes[source_of] - 1, limit - sizes[taker]) // 2
    room = jnp.where((source_of == ranking[0]) | (taker == ranking[0]) | (sizes[taker] == 0), 0, jnp.maximum(room, 0))
    moved = jax.random.randint(jax.random.fold_in(own, 4), (number_of // 2,), 0, 1 << 20) % (room + 1)
    sizes = sizes.at[source_of].add(-moved).at[taker].add(moved)
    members = jnp.searchsorted(jnp.cumsum(sizes), jnp.arange(rows * top), side="right").astype(jnp.int32)
    listing = members.reshape(top, rows).T
    listing = listing[jax.random.permutation(jax.random.fold_in(own, 1), rows)]
    offset_by = jax.random.randint(jax.random.fold_in(own, 2), (rows, 1), 0, top)
    return jnp.take_along_axis(listing, (jnp.arange(top)[None, :] + offset_by) % top, axis=1)


def shares(amount, total, reach, lean, full):
    weights = [(1 << 20) // math.isqrt(grade ** lean) + 1 for grade in range(1, amount + 1)]
    largest = reach if full else min(reach, max(-(-total // amount), total * weights[0] // sum(weights)))
    least = 1 if total - largest >= amount - 1 else 0
    counts, surplus = [largest] + [least] * (amount - 1), total - largest - least * (amount - 1)
    while surplus > 0:
        free = [i for i in range(1, amount) if counts[i] < largest] or [i for i in range(1, amount) if counts[i] < reach]
        pool, budget = sum([weights[i] for i in free]), surplus
        for i in free:
            extra = min(reach - counts[i], max(1, budget * weights[i] // pool), surplus)
            counts[i] = counts[i] + extra
            surplus = surplus - extra
    return np.array(counts)


def centred(own_key, shape, width, bound, cuts=(), held_as=jnp.bfloat16):
    array = jax.random.normal(own_key, shape, jnp.float32) * width
    if len(cuts) > 0:
        array = level_of(own_key, shape, cuts, -0.22, 0.18) * array
    return jnp.clip(array, min=-bound, max=bound).astype(held_as)


def setup_inputs(seed: int = 0) -> dict:
    key_list = jax.random.split(jax.random.key(seed), 7)
    tokens = centred(key_list[0], (TOKENS, D), 1.0, 6.0, ((0, 32),))
    expert_ids_keys = jax.random.split(jax.random.fold_in(key_list[1], 1), TOKENS // TOK_DEV)
    expert_ids_turns = jax.random.permutation(jax.random.fold_in(key_list[1], 3), TOKENS // TOK_DEV)
    expert_ids = jax.vmap(lambda own, number: routed_block(jax.random.fold_in(key_list[1], 2), own, number, TOK_DEV, EXPERTS, 2, CAP, 1))(expert_ids_keys, expert_ids_turns).reshape((TOKENS, 2))
    gates = jnp.clip(0.1 + 0.9 * jax.random.uniform(key_list[2], (TOKENS, 2), jnp.float32) ** level_of(key_list[2], (TOKENS, 2), ((0, 32),), -0.2, 0.2), 0.1, 1.0)
    w_in = centred(key_list[3], (EXPERTS, H, D), D ** -0.5, 0.15625, ((0, 4), (1, 8)))
    w_out = centred(key_list[4], (EXPERTS, H, D), H ** -0.5, 0.125, ((0, 4), (1, 8)))
    grad_y = centred(key_list[5], (TOKENS, D), 1.0, 6.0, ((0, 32),))
    return dict(tokens=tokens, expert_ids=expert_ids, gates=gates, w_in=w_in, w_out=w_out, grad_y=grad_y)


inv_sqrt_two = 0.7071067811865476
inv_sqrt_two_pi = 0.3989422804014327

def gelu_parts(values):
    cdf_part = 0.5 * (1.0 + jax.scipy.special.erf(values * inv_sqrt_two))
    return (values * cdf_part, cdf_part + values * jnp.exp(-0.5 * values * values) * inv_sqrt_two_pi)

def contract_first(left, right):
    return lax.dot_general(left, right, (((0,), (0,)), ((), ())), preferred_element_type=jnp.float32)

def contract_last(left, right):
    return lax.dot_general(left, right, (((1,), (1,)), ((), ())), preferred_element_type=jnp.float32)

def reference(tokens, expert_ids, gates, w_in, w_out, grad_y):
    flat_ids = expert_ids.reshape(-1).astype(jnp.int32)
    slot_total = flat_ids.shape[0]
    row_limit = N_EXP * N_FSDP * CAP
    slot_grad = (gates[:, :, None] * grad_y.astype(jnp.float32)[:, None, :]).astype(jnp.bfloat16)
    slot_grad = slot_grad.reshape(slot_total, D)

    def per_expert(carry, expert):
        out_slots, input_slots = carry
        row_index = jnp.nonzero(flat_ids == expert, size=row_limit, fill_value=slot_total)[0].astype(jnp.int32)
        is_live = row_index < slot_total
        safe_index = jnp.where(is_live, row_index, 0).astype(jnp.int32)
        rows_in = jnp.where(is_live[:, None], tokens[safe_index // 2], jnp.zeros((), jnp.bfloat16))
        grad_rows = jnp.where(is_live[:, None], slot_grad[safe_index], jnp.zeros((), jnp.bfloat16))
        weight_in = lax.dynamic_index_in_dim(w_in, expert, 0, keepdims=False)
        weight_out = lax.dynamic_index_in_dim(w_out, expert, 0, keepdims=False)
        hidden_pre = contract_last(rows_in, weight_in)
        act_full, slope_term = gelu_parts(hidden_pre)
        act_bf = act_full.astype(jnp.bfloat16)
        expert_out = jnp.dot(act_bf, weight_out, preferred_element_type=jnp.float32).astype(jnp.bfloat16)
        grad_act = contract_last(grad_rows, weight_out)
        grad_hidden = (grad_act * slope_term).astype(jnp.bfloat16)
        input_grad = jnp.dot(grad_hidden, weight_in, preferred_element_type=jnp.float32).astype(jnp.bfloat16)
        grad_in = contract_first(grad_hidden, rows_in)
        grad_out = contract_first(act_bf, grad_rows)
        out_slots = out_slots.at[row_index].set(expert_out, mode='drop')
        input_slots = input_slots.at[row_index].set(input_grad, mode='drop')
        return ((out_slots, input_slots), (grad_in, grad_out))
    start_carry = (jnp.zeros((slot_total, D), jnp.bfloat16), jnp.zeros((slot_total, D), jnp.bfloat16))
    (out_slots, input_slots), (grad_w_in, grad_w_out) = lax.scan(per_expert, start_carry, jnp.arange(EXPERTS, dtype=jnp.int32))
    out_three = out_slots.reshape(TOKENS, 2, D).astype(jnp.float32)
    mixed = lax.optimization_barrier(jnp.sum(gates[:, :, None] * out_three, axis=1)).astype(jnp.bfloat16)
    grad_gates = lax.optimization_barrier(jnp.sum(grad_y.astype(jnp.float32)[:, None, :] * out_three, axis=-1))
    grad_tokens = lax.optimization_barrier(jnp.sum(input_slots.reshape(TOKENS, 2, D).astype(jnp.float32), axis=1)).astype(jnp.bfloat16)
    return (mixed, grad_tokens, grad_w_in, grad_w_out, grad_gates)
```

```python
import jax
import jax.numpy as jnp
from jax import lax
from jax.sharding import PartitionSpec as P

inv_sqrt_two = 0.7071067811865476
inv_sqrt_two_pi = 0.3989422804014327
AXES = ("exp", "fsdp")
CORES = 2
DEPTH = 4


def gelu_parts(values):
    cdf_part = 0.5 * (1.0 + jax.scipy.special.erf(values * inv_sqrt_two))
    return (
        values * cdf_part,
        cdf_part + values * jnp.exp(-0.5 * values * values) * inv_sqrt_two_pi,
    )


def contract_first(left, right):
    return lax.dot_general(
        left, right, (((0,), (0,)), ((), ())), preferred_element_type=jnp.float32
    )


def contract_last(left, right):
    return lax.dot_general(
        left, right, (((1,), (1,)), ((), ())), preferred_element_type=jnp.float32
    )


class Grid:
    def __init__(self, n_exp, n_fsdp):
        self.nx, self.ny = n_exp // CORES, n_fsdp // DEPTH

    def move(self, array, to):
        pairs = []
        for x in range(self.nx):
            for c in range(CORES):
                for z in range(DEPTH):
                    for y in range(self.ny):
                        tx, tc, tz, ty = to(x, c, z, y)
                        pairs.append((self.index(x, c, z, y), self.index(tx, tc, tz, ty)))
        return lax.ppermute(array, AXES, pairs)

    def index(self, x, c, z, y):
        return ((x * CORES + c) * DEPTH + z) * self.ny + y

    def from_x(self, array, step):
        return self.move(array, lambda x, c, z, y: ((x - step) % self.nx, c, z, y))

    def from_y(self, array, step):
        return self.move(array, lambda x, c, z, y: (x, c, z, (y - step) % self.ny))

    def to_x(self, array, step):
        return self.move(array, lambda x, c, z, y: ((x + step) % self.nx, c, z, y))

    def to_y(self, array, step):
        return self.move(array, lambda x, c, z, y: (x, c, z, (y + step) % self.ny))

    def swap_core(self, array):
        return self.move(array, lambda x, c, z, y: (x, 1 - c, z, y))

    def swap_far(self, array):
        return self.move(array, lambda x, c, z, y: (x, c, z ^ 2, y))

    def swap_near(self, array):
        return self.move(array, lambda x, c, z, y: (x, c, z ^ 1, y))


def wide(array):
    return array.astype(jnp.float32)


def total(parts):
    out = wide(parts[0])
    for part in parts[1:]:
        out = out + wide(part)
    return out


def shards(tokens, expert_ids, gates, w_in, w_out, grad_y):
    rows, features = tokens.shape
    n_exp, n_fsdp = lax.axis_size("exp"), lax.axis_size("fsdp")
    grid = Grid(n_exp, n_fsdp)
    nx, ny = grid.nx, grid.ny
    hidden = w_in.shape[1]
    bf = jnp.bfloat16
    own_expert = lax.axis_index("exp")

    far_tokens, far_grads = grid.swap_far(tokens), grid.swap_far(grad_y)
    w_in, w_out = w_in[0], w_out[0]
    near_in, near_out = grid.swap_near(w_in), grid.swap_near(w_out)

    ids_row = expert_ids.T[None, :, :]
    named = ids_row == jnp.arange(n_exp, dtype=jnp.int32)[:, None, None]
    gate_rows = jnp.sum(jnp.where(named, gates.T[None], 0.0), axis=1)
    gate_rows = jnp.stack([gate_rows, grid.swap_far(gate_rows)])
    gate_rows = jnp.stack([gate_rows] + [grid.from_x(gate_rows, s) for s in range(1, nx)])
    gate_rows = jnp.stack([gate_rows] + [grid.from_y(gate_rows, s) for s in range(1, ny)])

    def spread_tokens(base):
        along = [base] + [grid.from_x(base, s) for s in range(1, nx)]
        return [along] + [[grid.from_y(part, s) for part in along] for s in range(1, ny)]

    def spread_grads(base):
        along = [base] + [grid.from_y(base, s) for s in range(1, ny)]
        return [[part] + [grid.from_x(part, s) for s in range(1, nx)] for part in along]

    def flat(table):
        return jnp.concatenate([part for line in table for part in line], axis=0)

    half_tokens = [flat(spread_tokens(base)) for base in (tokens, far_tokens)]
    half_grads = [flat(spread_grads(base)) for base in (grad_y, far_grads)]

    core_in, core_out = grid.swap_core(w_in), grid.swap_core(w_out)
    core_near_in, core_near_out = grid.swap_core(near_in), grid.swap_core(near_out)
    all_in = jnp.concatenate([w_in, near_in, core_in, core_near_in], axis=0)
    all_out = jnp.concatenate([w_out, near_out, core_out, core_near_out], axis=0)
    expert_pair = jnp.stack([own_expert, own_expert ^ 1])

    mixed_parts, input_parts, score_parts, acts, hiddens = [], [], [], [], []
    for half in range(2):
        scale = jnp.take(gate_rows[:, :, half], expert_pair, axis=2)
        scale = jnp.moveaxis(scale, 2, -1).reshape(-1, 2)
        pre = contract_last(half_tokens[half], all_in)
        act, slope = gelu_parts(pre)
        back = contract_last(half_grads[half], all_out)
        spread = jnp.repeat(scale, 2 * hidden, axis=1)
        act_scaled = (act * spread).astype(bf)
        grad_hidden = (back * slope * spread).astype(bf)
        score = jnp.sum((act * back).reshape(-1, 2, 2 * hidden), axis=-1)
        acts.append(act_scaled)
        hiddens.append(grad_hidden)
        score_parts.append(score)
        mixed_parts.append(jnp.dot(act_scaled, all_out, preferred_element_type=jnp.float32).astype(bf))
        input_parts.append(jnp.dot(grad_hidden, all_in, preferred_element_type=jnp.float32).astype(bf))

    def table(array):
        return array.reshape((ny, nx, rows) + array.shape[1:])

    def gather_yx(array):
        part = table(array)
        lines = [
            total([part[0, xo]] + [grid.to_y(part[s, xo], s) for s in range(1, ny)]).astype(array.dtype)
            for xo in range(nx)
        ]
        return total([lines[0]] + [grid.to_x(lines[s], s) for s in range(1, nx)]).astype(array.dtype)

    def gather_xy(array):
        part = table(array)
        lines = [
            total([part[yo, 0]] + [grid.to_x(part[yo, s], s) for s in range(1, nx)]).astype(array.dtype)
            for yo in range(ny)
        ]
        return total([lines[0]] + [grid.to_y(lines[s], s) for s in range(1, ny)]).astype(array.dtype)

    def home(parts, gather):
        far = grid.swap_far(gather(parts[1]))
        return wide(gather(parts[0])) + wide(far)

    mixed = home(mixed_parts, gather_yx).astype(bf)
    grad_tokens = home(input_parts, gather_xy).astype(bf)

    def score_of(score):
        row = jnp.zeros((n_exp, score.shape[0]), jnp.float32).at[expert_pair].set(score.T)
        return row.reshape(n_exp, ny, nx, rows)

    scores = jnp.stack([score_of(s) for s in score_parts], axis=1)
    scores = total([scores[:, :, 0]] + [grid.to_y(scores[:, :, s], s) for s in range(1, ny)])
    scores = total([scores[:, :, 0]] + [grid.to_x(scores[:, :, s], s) for s in range(1, nx)])
    scores = scores[:, 0] + grid.swap_far(scores[:, 1])
    picked = jnp.sum(jnp.where(named, scores[:, None, :], 0.0), axis=0)
    grad_gates = picked.T

    both_tokens = jnp.concatenate(half_tokens, axis=0)
    both_grads = jnp.concatenate(half_grads, axis=0)
    both_acts = jnp.concatenate(acts, axis=0)
    both_hiddens = jnp.concatenate(hiddens, axis=0)
    span = 2 * hidden

    def weight_grad(left, right):
        other = contract_first(left[:, span:], right).astype(bf)
        mine = contract_first(left[:, :span], right)
        both = mine + wide(grid.swap_core(other))
        return both[:hidden] + wide(grid.swap_near(both[hidden:].astype(bf)))

    grad_in = weight_grad(both_hiddens, both_tokens)
    grad_out = weight_grad(both_acts, both_grads)
    return (mixed, grad_tokens, grad_in[None], grad_out[None], grad_gates)


def solution(mesh):
    rows = P(AXES, None)
    weights = P("exp", "fsdp", None)
    return jax.shard_map(
        shards,
        mesh=mesh,
        in_specs=(rows, rows, rows, weights, weights, rows),
        out_specs=(rows, rows, weights, weights, rows),
        check_vma=False,
    )
```

```python
import jax
import jax.numpy as jnp
from jax import lax
from jax.sharding import PartitionSpec as P

inv_sqrt_two = 0.7071067811865476
inv_sqrt_two_pi = 0.3989422804014327
AXES = ("exp", "fsdp")
CORES = 2
DEPTH = 4


def gelu_parts(values):
    cdf_part = 0.5 * (1.0 + jax.scipy.special.erf(values * inv_sqrt_two))
    return (
        values * cdf_part,
        cdf_part + values * jnp.exp(-0.5 * values * values) * inv_sqrt_two_pi,
    )


def contract_first(left, right):
    return lax.dot_general(
        left, right, (((0,), (0,)), ((), ())), preferred_element_type=jnp.float32
    )


def contract_last(left, right):
    return lax.dot_general(
        left, right, (((1,), (1,)), ((), ())), preferred_element_type=jnp.float32
    )


class Grid:
    def __init__(self, n_exp, n_fsdp):
        self.nx, self.ny = n_exp // CORES, n_fsdp // DEPTH

    def move(self, array, to):
        pairs = []
        for x in range(self.nx):
            for c in range(CORES):
                for z in range(DEPTH):
                    for y in range(self.ny):
                        tx, tc, tz, ty = to(x, c, z, y)
                        pairs.append((self.index(x, c, z, y), self.index(tx, tc, tz, ty)))
        return lax.ppermute(array, AXES, pairs)

    def index(self, x, c, z, y):
        return ((x * CORES + c) * DEPTH + z) * self.ny + y

    def from_x(self, array, step):
        return self.move(array, lambda x, c, z, y: ((x - step) % self.nx, c, z, y))

    def from_y(self, array, step):
        return self.move(array, lambda x, c, z, y: (x, c, z, (y - step) % self.ny))

    def to_x(self, array, step):
        return self.move(array, lambda x, c, z, y: ((x + step) % self.nx, c, z, y))

    def to_y(self, array, step):
        return self.move(array, lambda x, c, z, y: (x, c, z, (y + step) % self.ny))

    def swap_core(self, array):
        return self.move(array, lambda x, c, z, y: (x, 1 - c, z, y))

    def swap_far(self, array):
        return self.move(array, lambda x, c, z, y: (x, c, z ^ 2, y))

    def swap_near(self, array):
        return self.move(array, lambda x, c, z, y: (x, c, z ^ 1, y))


def wide(array):
    return array.astype(jnp.float32)


def total(parts):
    out = wide(parts[0])
    for part in parts[1:]:
        out = out + wide(part)
    return out


def tie(*groups):
    return lax.optimization_barrier(groups)


def shards(tokens, expert_ids, gates, w_in, w_out, grad_y):
    rows, features = tokens.shape
    n_exp, n_fsdp = lax.axis_size("exp"), lax.axis_size("fsdp")
    grid = Grid(n_exp, n_fsdp)
    nx, ny = grid.nx, grid.ny
    hidden = w_in.shape[1]
    bf = jnp.bfloat16
    own_expert = lax.axis_index("exp")

    far = jnp.concatenate([tokens, grad_y], axis=0)
    far, tokens, grad_y = tie(far, tokens, grad_y)
    far = grid.swap_far(far)
    own_weights = jnp.concatenate([w_in[0], w_out[0]], axis=0)
    near_weights = grid.swap_near(own_weights)

    ids_row = expert_ids.T[None, :, :]
    named = ids_row == jnp.arange(n_exp, dtype=jnp.int32)[:, None, None]
    gate_rows = jnp.sum(jnp.where(named, gates.T[None], 0.0), axis=1)

    def tok_first(tok):
        return [tok] + [grid.from_x(tok, s) for s in range(1, nx)]

    def grad_first(grad):
        return [grad] + [grid.from_y(grad, s) for s in range(1, ny)]

    def tok_second(line):
        line = jnp.concatenate(line, axis=0)
        return jnp.concatenate([line] + [grid.from_y(line, s) for s in range(1, ny)], axis=0)

    def grad_second(line):
        line = jnp.concatenate(line, axis=0)
        pieces = [line] + [grid.from_x(line, s) for s in range(1, nx)]
        return jnp.concatenate(
            [pieces[xo][yo * rows : (yo + 1) * rows] for yo in range(ny) for xo in range(nx)],
            axis=0,
        )

    gates_y = jnp.stack([gate_rows] + [grid.from_y(gate_rows, s) for s in range(1, ny)])
    tok_line, grad_line, gates_y = tie(tok_first(tokens), grad_first(grad_y), gates_y)
    gates_x = jnp.stack([gates_y] + [grid.from_x(gates_y, s) for s in range(1, nx)], axis=1)
    near_half = (tok_second(tok_line), grad_second(grad_line))
    far, gates_x = tie(far, gates_x)
    far_tok, far_grad = tok_first(far[:rows]), grad_first(far[rows:])
    near_half, gates_x, own_weights = tie(near_half, gates_x, own_weights)
    gates_z = jnp.stack([gates_x, grid.swap_far(gates_x)], axis=2)
    other_own = grid.swap_core(own_weights)
    far_tok, far_grad, other_own = tie(far_tok, far_grad, other_own)
    far_half = (tok_second(far_tok), grad_second(far_grad))
    halves = (near_half, far_half)

    other_near, gates_z = tie(grid.swap_core(near_weights), gates_z)
    four = (own_weights, near_weights, other_own, other_near)
    all_in = jnp.concatenate([part[:hidden] for part in four], axis=0)
    all_out = jnp.concatenate([part[hidden:] for part in four], axis=0)
    expert_pair = jnp.stack([own_expert, own_expert ^ 1])
    span = 2 * hidden
    pair_gates = jnp.take(gates_z, expert_pair, axis=3)

    def mixed_first(array):
        line = array.reshape(ny, nx * rows, features)
        return [line[0]] + [grid.to_y(line[s], s) for s in range(1, ny)]

    def mixed_second(line):
        line = total(line).astype(bf).reshape(nx, rows, features)
        return [line[0]] + [grid.to_x(line[s], s) for s in range(1, nx)]

    def input_first(array):
        part = array.reshape(ny, nx, rows, features)
        line = [part[:, s].reshape(ny * rows, features) for s in range(nx)]
        return [line[0]] + [grid.to_x(line[s], s) for s in range(1, nx)]

    def input_second(line):
        line = total(line).astype(bf).reshape(ny, rows, features)
        return [line[0]] + [grid.to_y(line[s], s) for s in range(1, ny)]

    mixed_parts, input_parts, acts, hiddens, products = [], [], [], [], []
    for half in range(2):
        tok, grad = halves[half]
        if half == 1:
            near_mixed, near_input = mixed_first(mixed_parts[0]), input_first(input_parts[0])
        scale = [pair_gates[:, :, half, e].reshape(-1, 1) for e in range(2)]
        pre = contract_last(tok, all_in)
        act, slope = gelu_parts(pre)
        back = contract_last(grad, all_out)
        column = lax.broadcasted_iota(jnp.int32, (1, 2 * span), 1)
        factor = jnp.where(column < span, scale[0], scale[1])
        act_scaled = (act * factor).astype(bf)
        grad_hidden = (back * slope * factor).astype(bf)
        products.append(act * back)
        acts.append(act_scaled)
        hiddens.append(grad_hidden)
        mixed_parts.append(jnp.dot(act_scaled, all_out, preferred_element_type=jnp.float32).astype(bf))
        input_parts.append(jnp.dot(grad_hidden, all_in, preferred_element_type=jnp.float32).astype(bf))

    far_mixed, far_input = mixed_first(mixed_parts[1]), input_first(input_parts[1])

    both_tokens = jnp.concatenate([half[0] for half in halves], axis=0)
    both_grads = jnp.concatenate([half[1] for half in halves], axis=0)
    both_acts = jnp.concatenate(acts, axis=0)
    both_hiddens = jnp.concatenate(hiddens, axis=0)
    other = jnp.concatenate(
        [
            contract_first(both_hiddens[:, span:], both_tokens).astype(bf),
            contract_first(both_acts[:, span:], both_grads).astype(bf),
        ],
        axis=0,
    )
    other = grid.swap_core(other)
    other = wide(other)
    sum_in = contract_first(both_hiddens[:, :span], both_tokens) + other[:span]
    sum_out = contract_first(both_acts[:, :span], both_grads) + other[span:]

    near_sums = jnp.concatenate([sum_in[hidden:], sum_out[hidden:]], axis=0).astype(bf)
    far_mixed, far_input, near_mixed, near_input, near_sums = tie(
        far_mixed, far_input, near_mixed, near_input, near_sums
    )
    far_mixed, far_input = mixed_second(far_mixed), input_second(far_input)
    near_mixed, near_input = mixed_second(near_mixed), input_second(near_input)
    near_sums = wide(grid.swap_near(near_sums))

    scores = jnp.stack(
        [
            jnp.sum(p[:, e * span : (e + 1) * span], axis=1).reshape(ny, nx, rows)
            for p in products
            for e in range(2)
        ],
        axis=2,
    ).reshape(ny, nx, 2, 2, rows)
    experts = jnp.arange(n_exp, dtype=jnp.int32)[:, None]
    scores = sum(
        jnp.where(experts == expert_pair[e], scores[:, :, :, e][:, :, :, None, :], 0.0)
        for e in range(2)
    )
    scores = scores[:, :, 0] + grid.swap_far(scores[:, :, 1])
    scores = total([scores[0]] + [grid.to_y(scores[s], s) for s in range(1, ny)])
    scores = total([scores[0]] + [grid.to_x(scores[s], s) for s in range(1, nx)])
    grad_gates = jnp.sum(jnp.where(named, scores[:, None, :], 0.0), axis=0).T

    far_sums = jnp.concatenate([total(far_mixed), total(far_input)], axis=0).astype(bf)
    far_sums = wide(grid.swap_far(far_sums))
    mixed = (total(near_mixed) + far_sums[:rows]).astype(bf)
    grad_tokens = (total(near_input) + far_sums[rows:]).astype(bf)
    grad_in = sum_in[:hidden] + near_sums[:hidden]
    grad_out = sum_out[:hidden] + near_sums[hidden:]
    return (mixed, grad_tokens, grad_in[None], grad_out[None], grad_gates)


def solution(mesh):
    rows = P(AXES, None)
    weights = P("exp", "fsdp", None)
    return jax.shard_map(
        shards,
        mesh=mesh,
        in_specs=(rows, rows, rows, weights, weights, rows),
        out_specs=(rows, rows, weights, weights, rows),
        check_vma=False,
    )
```

```python
import functools

import jax
import jax.numpy as jnp
from jax import lax
from jax.experimental import pallas as pl
from jax.experimental.pallas import tpu as pltpu
from jax.sharding import PartitionSpec as P

inv_sqrt_two = 0.7071067811865476
inv_sqrt_two_pi = 0.3989422804014327
AXES = ("exp", "fsdp")
CORES = 2
DEPTH = 4


def contract_first(left, right):
    return lax.dot_general(
        left, right, (((0,), (0,)), ((), ())), preferred_element_type=jnp.float32
    )


def contract_last(left, right):
    return lax.dot_general(
        left, right, (((1,), (1,)), ((), ())), preferred_element_type=jnp.float32
    )


def gelu_parts(values):
    cdf_part = 0.5 * (1.0 + lax.erf(values * inv_sqrt_two))
    return (
        values * cdf_part,
        cdf_part + values * jnp.exp(-0.5 * values * values) * inv_sqrt_two_pi,
    )


class Copies:
    def __init__(self, sems):
        self.sems, self.all = sems, []

    def start(self, source, target):
        copy = pltpu.make_async_copy(source, target, self.sems.at[len(self.all)])
        copy.start()
        self.all.append(copy)
        return copy


def hidden_part(tok, grad, weight, scale, act_ref, hid_ref, columns):
    hidden = weight.shape[0] // 2
    pre = contract_last(tok, weight[:hidden, :])
    back = contract_last(grad, weight[hidden:, :])
    full, slope = gelu_parts(pre)
    act_ref[:, columns] = (full * scale).astype(jnp.bfloat16)
    hid_ref[:, columns] = (back * slope * scale).astype(jnp.bfloat16)
    return jnp.sum(full * back, axis=1, keepdims=True)


def gate_of(gate, expert):
    here = lax.broadcasted_iota(jnp.int32, gate.shape, 1) == expert
    return here, jnp.sum(jnp.where(here, gate, 0.0), axis=1, keepdims=True)


def decode(code, rows):
    wide_code = code.astype(jnp.float32)
    return (wide_code[:, :rows] + wide_code[:, rows:]).T


def far_kernel(plan, *refs):
    count, rows = plan
    refs = list(refs)
    take = lambda number: [refs.pop(0) for _ in range(number)]
    (first_ref,), pieces, weights_in = take(1), take(count), take(4)
    (act_out, hid_out), pieces_out = take(2), take(count)
    (tok, grad, coded_rows, extra), values = take(4), take(2)
    weights, stages, (sems_in, sems_out) = take(4), take(2), take(2)
    hidden = weights[0].shape[0] // 2
    tile = 2 * rows
    loads, stores = Copies(sems_in), Copies(sems_out)
    weight_ready, ready = [loads.start(weights_in[0], weights[0])], []

    def load_tile(t):
        group = []
        for b in (2 * t, 2 * t + 1):
            at = pl.ds(b * rows, rows)
            group.append(loads.start(pieces[b].at[pl.ds(0, rows)], tok.at[at]))
            group.append(loads.start(pieces[b].at[pl.ds(rows, rows)], grad.at[at]))
            source = pieces[b].at[pl.ds(2 * rows, SPARE), pl.ds(0, 2 * rows)]
            group.append(loads.start(source, coded_rows.at[b]))
        ready.append(group)

    load_tile(0)
    for i in range(1, 4):
        weight_ready.append(loads.start(weights_in[i], weights[i]))
    for t in range(1, count // 2):
        load_tile(t)
    first = first_ref[0]
    extra[...] = jnp.zeros_like(extra)
    staged, pending = [[], []], []
    for t in range(count // 2):
        span = pl.ds(t * tile, tile)
        for copy in ready[t]:
            copy.wait()
        gate = jnp.concatenate([decode(coded_rows[2 * t + k], rows) for k in range(2)], axis=0)
        total = 0.0
        for e in range(2):
            here, scale = gate_of(gate, first ^ e)
            part = 0.0
            for i in (2 * e, 2 * e + 1):
                if t == 0:
                    weight_ready[i].wait()
                part = part + hidden_part(
                    tok[span, :],
                    grad[span, :],
                    weights[i],
                    scale,
                    values[0].at[span],
                    values[1].at[span],
                    slice(i * hidden, (i + 1) * hidden),
                )
            total = total + jnp.where(here, part, 0.0)
        for value, target in zip(values, (act_out, hid_out)):
            source = value.at[span, pl.ds(0, 2 * hidden)]
            pending.append(stores.start(source, target.at[span]))
        for k in range(2):
            b = 2 * t + k
            encode(total[k * rows : (k + 1) * rows, :], extra, b, rows)
            pending.append(stores.start(extra.at[b], pieces_out[b].at[pl.ds(2 * rows, SPARE)]))
        for copy in staged[t % 2]:
            copy.wait()
        staged[t % 2] = []
        for kind, (stage, low) in enumerate(zip(stages, (hidden, 0))):
            lefts = [values[kind].at[span, pl.ds(i * hidden, hidden)] for i in range(4)]
            stage[t % 2] = partial_output(lefts, weights, low)
            for k in range(2):
                source = stage.at[t % 2, pl.ds(k * rows, rows)]
                target = pieces_out[2 * t + k].at[pl.ds(kind * rows, rows)]
                staged[t % 2].append(stores.start(source, target))
    for copy in pending + staged[0] + staged[1]:
        copy.wait()


def encode(score, extra, b, rows):
    rest = score.T
    high = rest.astype(jnp.bfloat16)
    extra[b, :, pl.ds(0, rows)] = high
    extra[b, :, pl.ds(rows, rows)] = (rest - high.astype(jnp.float32)).astype(jnp.bfloat16)


def partial_output(lefts, weights, low):
    hidden = weights[0].shape[0] // 2
    out = 0.0
    for left, weight in zip(lefts, weights):
        out = out + jnp.dot(
            left[...], weight[low : low + hidden, :], preferred_element_type=jnp.float32
        )
    return out.astype(jnp.bfloat16)


def split(stack, count, rows):
    step = 2 * rows + SPARE
    return [stack.at[pl.ds(b * step, step)] for b in range(count)]


def load_blocks(loads, blocks, slot, tok, grad, coded_rows, rows):
    started = []
    for k, block in enumerate(blocks):
        at = pl.ds(k * rows, rows)
        started.append(loads.start(block.at[pl.ds(0, rows)], tok.at[slot, at]))
        started.append(loads.start(block.at[pl.ds(rows, rows)], grad.at[slot, at]))
        if coded_rows is not None:
            source = block.at[pl.ds(2 * rows, SPARE), pl.ds(0, 2 * rows)]
            started.append(loads.start(source, coded_rows.at[slot, k]))
    return started


def add_sums(totals, acts, hids, tok, grad, slot, empty, results=None):
    hidden = totals.shape[1]
    for which, (left, right) in enumerate(((hids, tok), (acts, grad))):
        for k in range(2):
            out = contract_first(left[slot, :, k * hidden : (k + 1) * hidden], right[slot])
            if not empty:
                out = out + totals[2 * which + k]
            if results is None or k == 0:
                totals[2 * which + k] = out
            else:
                results[which] = out.astype(jnp.bfloat16)


def sums_kernel(plan, *refs):
    count, rows = plan
    refs = list(refs)
    take = lambda number: [refs.pop(0) for _ in range(number)]
    (first_ref,), near, far, (near_over,) = take(1), take(count), take(count), take(1)
    far_over, far_values = take(count), take(2)
    weights_in, near_values, keep_out, near_sums, (score,) = take(2), take(2), take(2), take(2), take(1)
    tok, grad, coded_rows, acts, hids, totals, results = take(7)
    weights, (sems_in, sems_out) = take(2), take(2)
    group = 4
    tile = group * rows
    hidden = weights[0].shape[0] // 2
    loads, stores = Copies(sems_in), Copies(sems_out)
    lists = [near, far, split(near_over, count, rows), far_over]
    steps = [
        (kind, g, blocks[g * group : (g + 1) * group])
        for kind, blocks in enumerate(lists)
        for g in range(count // group)
    ]

    def load(n):
        kind, g, blocks = steps[n]
        codes = None if kind == 1 else coded_rows
        started = load_blocks(loads, blocks, n % 2, tok, grad, codes, rows)
        if kind == 1:
            for source, target in zip(far_values, (acts, hids)):
                source = source.at[pl.ds(g * tile, tile)]
                started.append(loads.start(source, target.at[n % 2]))
        return started

    weight_ready = [loads.start(weights_in[0], weights[0])]
    ready = load(0)
    weight_ready.append(loads.start(weights_in[1], weights[1]))
    first = first_ref[0]
    saved = [[], []]
    for n, (kind, g, blocks) in enumerate(steps):
        slot = n % 2
        for copy in saved[1 - slot]:
            copy.wait()
        saved[1 - slot] = []
        coming = load(n + 1) if n + 1 < len(steps) else []
        for copy in ready:
            copy.wait()
        ready = coming
        if kind != 1:
            gate = jnp.concatenate([decode(coded_rows[slot, k], rows) for k in range(group)], axis=0)
            here, scale = gate_of(gate, first)
            part = 0.0
            for k in range(2):
                if n == 0:
                    weight_ready[k].wait()
                columns = slice(k * hidden, (k + 1) * hidden)
                part = part + hidden_part(
                    tok[slot], grad[slot], weights[k], scale, acts.at[slot], hids.at[slot], columns
                )
        if kind == 0:
            span = pl.ds(g * tile, tile)
            score[span, :] = jnp.where(here, part, 0.0)
            saved[slot] = [
                stores.start(acts.at[slot], near_values[0].at[span]),
                stores.start(hids.at[slot], near_values[1].at[span]),
            ]
        last = n + 1 == len(steps)
        add_sums(totals, acts, hids, tok, grad, slot, n == 0, results if last else None)
    tail = [stores.start(totals.at[2 * which], keep_out[which]) for which in range(2)]
    tail += [stores.start(results.at[which], near_sums[which]) for which in range(2)]
    for copy in saved[0] + saved[1] + tail:
        copy.wait()


def near_kernel(plan, *refs):
    count, rows = plan
    refs = list(refs)
    take = lambda number: [refs.pop(0) for _ in range(number)]
    (first_ref, score), near, values_in, weights_in = take(2), take(count), take(2), take(4)
    pieces_out = take(count)
    tok, grad, coded_rows, extra, acts, hids, others, outs = take(8)
    weights, (sems_in, sems_out) = take(4), take(2)
    hidden = weights[0].shape[0] // 2
    group = 4
    tile = group * rows
    loads, stores = Copies(sems_in), Copies(sems_out)

    def load(g):
        blocks, span = near[g * group : (g + 1) * group], pl.ds(g * tile, tile)
        started = load_blocks(loads, blocks, g % 2, tok, grad, coded_rows, rows)
        for source, target in zip(values_in, (acts, hids)):
            started.append(loads.start(source.at[span], target.at[g % 2]))
        return started

    weight_ready = {2: loads.start(weights_in[2], weights[2])}
    ready = load(0)
    for i in (3, 0, 1):
        weight_ready[i] = loads.start(weights_in[i], weights[i])
    first = first_ref[0]
    extra[...] = jnp.zeros_like(extra)
    out_copies = []
    for g in range(count // group):
        slot = g % 2
        coming = load(g + 1) if (g + 1) * group < count else []
        for copy in ready + out_copies:
            copy.wait()
        ready, out_copies = coming, []
        gate = jnp.concatenate([decode(coded_rows[slot, k], rows) for k in range(group)], axis=0)
        here, scale = gate_of(gate, first ^ 1)
        part = 0.0
        for k in range(2):
            if g == 0:
                weight_ready[2 + k].wait()
            columns = slice(k * hidden, (k + 1) * hidden)
            part = part + hidden_part(
                tok[slot], grad[slot], weights[2 + k], scale, others.at[0], others.at[1], columns
            )
        total = score[pl.ds(g * tile, tile), :] + jnp.where(here, part, 0.0)
        if g == 0:
            weight_ready[0].wait()
            weight_ready[1].wait()
        for k in range(group):
            b = g * group + k
            encode(total[k * rows : (k + 1) * rows, :], extra, b, rows)
            out_copies.append(stores.start(extra.at[b], pieces_out[b].at[pl.ds(2 * rows, SPARE)]))
        for which, (mine, low) in enumerate(((acts, hidden), (hids, 0))):
            lefts = [mine.at[slot, :, pl.ds(k * hidden, hidden)] for k in range(2)]
            lefts += [others.at[which, :, pl.ds(k * hidden, hidden)] for k in range(2)]
            outs[which] = partial_output(lefts, weights, low)
            for k in range(group):
                source = outs.at[which, pl.ds(k * rows, rows)]
                target = pieces_out[g * group + k].at[pl.ds(which * rows, rows)]
                out_copies.append(stores.start(source, target))
    for copy in out_copies:
        copy.wait()


ANYWHERE = pl.BlockSpec(memory_space=pl.ANY)
IN_VMEM = pl.BlockSpec(memory_space=pltpu.VMEM)
IN_SMEM = pl.BlockSpec(memory_space=pltpu.SMEM)
SPARE = 16


def kernel_params(flops=10**11):
    return dict(
        compiler_params=pltpu.CompilerParams(vmem_limit_bytes=58 * 2**20),
        cost_estimate=pl.CostEstimate(flops=flops, bytes_accessed=flops // 10**3, transcendentals=0),
    )


def far_call(rows, first, pieces, weights):
    count, features = len(pieces), pieces[0].shape[1]
    hidden = weights[0].shape[0] // 2
    height = count * rows
    bf = jnp.bfloat16
    shape = jax.ShapeDtypeStruct
    outs = pl.pallas_call(
        functools.partial(far_kernel, (count, rows)),
        out_shape=[shape((height, 2 * hidden), bf)] * 2
        + [shape((2 * rows + SPARE, features), bf)] * count,
        in_specs=[IN_SMEM] + [ANYWHERE] * (count + 4),
        out_specs=[ANYWHERE] * (2 + count),
        scratch_shapes=[pltpu.VMEM((height, features), bf)] * 2
        + [pltpu.VMEM((count, SPARE, 2 * rows), bf)]
        + [pltpu.VMEM((count, SPARE, features), bf)]
        + [pltpu.VMEM((height, 4 * hidden), bf)] * 2
        + [pltpu.VMEM((2 * hidden, features), bf)] * 4
        + [pltpu.VMEM((2, 2 * rows, features), bf)] * 2
        + [pltpu.SemaphoreType.DMA((3 * count + 4,)), pltpu.SemaphoreType.DMA((4 * count,))],
        **kernel_params(),
    )(first, *pieces, *weights)
    return outs[:2], outs[2:]


def sums_call(rows, first, near, far, near_over, far_over, far_values, weights):
    count, features = len(near), near[0].shape[1]
    hidden = weights[0].shape[0] // 2
    height, tile = count * rows, 4 * rows
    bf, f32 = jnp.bfloat16, jnp.float32
    shape = jax.ShapeDtypeStruct
    outs = pl.pallas_call(
        functools.partial(sums_kernel, (count, rows)),
        out_shape=[shape((height, 2 * hidden), bf)] * 2
        + [shape((hidden, features), f32)] * 2
        + [shape((hidden, features), bf)] * 2
        + [shape((height, SPARE), f32)],
        in_specs=[IN_SMEM] + [ANYWHERE] * (3 * count + 5),
        out_specs=[ANYWHERE] * 6 + [IN_VMEM],
        scratch_shapes=[pltpu.VMEM((2, tile, features), bf)] * 2
        + [pltpu.VMEM((2, 4, SPARE, 2 * rows), bf)]
        + [pltpu.VMEM((2, tile, 2 * hidden), bf)] * 2
        + [pltpu.VMEM((4, hidden, features), f32)]
        + [pltpu.VMEM((2, hidden, features), bf)]
        + [pltpu.VMEM((2 * hidden, features), bf)] * 2
        + [pltpu.SemaphoreType.DMA((12 * count + 2,)), pltpu.SemaphoreType.DMA((count + 4,))],
        **kernel_params(),
    )(first, *near, *far, near_over, *far_over, *far_values, *weights)
    return outs[:2], outs[2:4], outs[4:6], outs[6]


def near_call(rows, first, score, near, values, weights):
    count, features = len(near), near[0].shape[1]
    hidden = weights[0].shape[0] // 2
    tile = 4 * rows
    bf = jnp.bfloat16
    return pl.pallas_call(
        functools.partial(near_kernel, (count, rows)),
        out_shape=[jax.ShapeDtypeStruct((2 * rows + SPARE, features), bf)] * count,
        in_specs=[IN_SMEM, IN_VMEM] + [ANYWHERE] * (count + 6),
        out_specs=[ANYWHERE] * count,
        scratch_shapes=[pltpu.VMEM((2, tile, features), bf)] * 2
        + [pltpu.VMEM((2, 4, SPARE, 2 * rows), bf)]
        + [pltpu.VMEM((count, SPARE, features), bf)]
        + [pltpu.VMEM((2, tile, 2 * hidden), bf)] * 3
        + [pltpu.VMEM((2, tile, features), bf)]
        + [pltpu.VMEM((2 * hidden, features), bf)] * 4
        + [pltpu.SemaphoreType.DMA((4 * count + 4,)), pltpu.SemaphoreType.DMA((3 * count,))],
        **kernel_params(1000),
    )(first, score, *near, *values, *weights)


def coded(rows_of, features):
    high = lax.reduce_precision(rows_of, 8, 7)
    both = jnp.concatenate([high, rows_of - high], axis=1).astype(jnp.bfloat16)
    return jnp.pad(both, ((0, SPARE - both.shape[0]), (0, features - both.shape[1])))


class Grid:
    def __init__(self, n_exp, n_fsdp):
        self.nx, self.ny = n_exp // CORES, n_fsdp // DEPTH

    def move(self, array, to):
        pairs = []
        for x in range(self.nx):
            for c in range(CORES):
                for z in range(DEPTH):
                    for y in range(self.ny):
                        tx, tc, tz, ty = to(x, c, z, y)
                        pairs.append((self.index(x, c, z, y), self.index(tx, tc, tz, ty)))
        return lax.ppermute(array, AXES, pairs)

    def index(self, x, c, z, y):
        return ((x * CORES + c) * DEPTH + z) * self.ny + y

    def spread(self, array, dx, dy):
        if dx == dy == 0:
            return array
        return self.move(
            array, lambda x, c, z, y: ((x - dx) % self.nx, c, z, (y - dy) % self.ny)
        )

    def collect(self, array, dx, dy):
        if dx == dy == 0:
            return array
        return self.move(
            array, lambda x, c, z, y: ((x + dx) % self.nx, c, z, (y + dy) % self.ny)
        )

    def swap_core(self, array):
        return self.move(array, lambda x, c, z, y: (x, 1 - c, z, y))

    def swap_far(self, array):
        return self.move(array, lambda x, c, z, y: (x, c, z ^ 2, y))

    def swap_near(self, array):
        return self.move(array, lambda x, c, z, y: (x, c, z ^ 1, y))


def wide(array):
    return array.astype(jnp.float32)


def total(parts):
    out = wide(parts[0])
    for part in parts[1:]:
        out = out + wide(part)
    return out


def tie(*groups):
    return lax.optimization_barrier(groups)


def shards(tokens, expert_ids, gates, w_in, w_out, grad_y):
    rows, features = tokens.shape
    n_exp, n_fsdp = lax.axis_size("exp"), lax.axis_size("fsdp")
    grid = Grid(n_exp, n_fsdp)
    steps = [(xo, yo) for yo in range(grid.ny) for xo in range(grid.nx)]
    bf = jnp.bfloat16
    first = jnp.reshape(lax.axis_index("exp"), (1,))

    ids_row = expert_ids.T[None, :, :]
    named = ids_row == jnp.arange(n_exp, dtype=jnp.int32)[:, None, None]
    gate_rows = jnp.sum(jnp.where(named, gates.T[None], 0.0), axis=1)

    own = jnp.concatenate([tokens, grad_y, coded(gate_rows, features)], axis=0)
    far = grid.swap_far(own)
    own_weights = jnp.concatenate([w_in[0], w_out[0]], axis=0)
    near_weights = grid.swap_near(own_weights)
    near_pieces = [grid.spread(own, *step) for step in steps]
    near_pieces, far, core_weights = tie(near_pieces, far, own_weights)
    far_pieces = [grid.spread(far, *step) for step in steps]
    near_over = grid.swap_core(jnp.concatenate(near_pieces, axis=0))
    other_own = grid.swap_core(core_weights)
    far_pieces, other_own = tie(far_pieces, other_own)
    other_near = grid.swap_core(near_weights)
    weights = [own_weights, near_weights, other_own, other_near]
    far_values, far_out = far_call(rows, first, far_pieces, weights)

    far_home = [grid.collect(part, *step) for part, step in zip(far_out, steps)]
    far_over = [grid.swap_core(piece) for piece in far_pieces]
    near_values, keep, near_sums, score = sums_call(
        rows, first, near_pieces, far_pieces, near_over, far_over, far_values, weights[:2]
    )
    near_out = near_call(rows, first, score, near_pieces, near_values, weights)
    far_home, near_out, _ = tie(far_home, near_out, near_sums)
    near_sums = [grid.swap_near(part) for part in near_sums]
    far_home = total(far_home)

    def score_of(home):
        return home[2 * rows :, :rows] + home[2 * rows :, rows : 2 * rows]

    far_home = jnp.concatenate(
        [far_home[: 2 * rows].astype(bf), coded(score_of(far_home), features)], axis=0
    )
    far_home = grid.swap_far(far_home)
    near_home = total([grid.collect(part, *step) for part, step in zip(near_out, steps)])

    home = near_home + wide(far_home)
    mixed, grad_tokens = home[:rows].astype(bf), home[rows : 2 * rows].astype(bf)
    score = score_of(home)[:n_exp]
    grad_gates = jnp.sum(jnp.where(named, score[:, None, :], 0.0), axis=0).T
    grad_in, grad_out = [mine + wide(theirs) for mine, theirs in zip(keep, near_sums)]
    return (mixed, grad_tokens, grad_in[None], grad_out[None], grad_gates)


def solution(mesh):
    rows = P(AXES, None)
    weights = P("exp", "fsdp", None)
    return jax.shard_map(
        shards,
        mesh=mesh,
        in_specs=(rows, rows, rows, weights, weights, rows),
        out_specs=(rows, rows, weights, weights, rows),
        check_vma=False,
    )
```

```python
import functools

import jax
import jax.numpy as jnp
from jax import lax
from jax.experimental import pallas as pl
from jax.experimental.pallas import tpu as pltpu
from jax.sharding import PartitionSpec as P

inv_sqrt_two = 0.7071067811865476
inv_sqrt_two_pi = 0.3989422804014327
AXES = ("exp", "fsdp")
CORES = 2
DEPTH = 4


def contract_first(left, right):
    return lax.dot_general(
        left, right, (((0,), (0,)), ((), ())), preferred_element_type=jnp.float32
    )


def contract_last(left, right):
    return lax.dot_general(
        left, right, (((1,), (1,)), ((), ())), preferred_element_type=jnp.float32
    )


def gelu_parts(values):
    cdf_part = 0.5 * (1.0 + lax.erf(values * inv_sqrt_two))
    return (
        values * cdf_part,
        cdf_part + values * jnp.exp(-0.5 * values * values) * inv_sqrt_two_pi,
    )


class Copies:
    def __init__(self, sems):
        self.sems, self.all = sems, []

    def start(self, source, target):
        copy = pltpu.make_async_copy(source, target, self.sems.at[len(self.all)])
        copy.start()
        self.all.append(copy)
        return copy

    def pair(self, sources, target):
        hidden = target.shape[0] // 2
        return Both(
            [self.start(sources[k], target.at[pl.ds(k * hidden, hidden)]) for k in range(2)]
        )


class Both:
    def __init__(self, copies):
        self.copies = copies

    def wait(self):
        for copy in self.copies:
            copy.wait()


def hidden_part(tok, grad, weight, scale, act_ref, hid_ref, columns):
    hidden = weight.shape[0] // 2
    pre = contract_last(tok, weight[:hidden, :])
    back = contract_last(grad, weight[hidden:, :])
    full, slope = gelu_parts(pre)
    act_ref[:, columns] = (full * scale).astype(jnp.bfloat16)
    hid_ref[:, columns] = (back * slope * scale).astype(jnp.bfloat16)
    return jnp.sum(full * back, axis=1, keepdims=True)


def gate_of(gate, expert):
    here = lax.broadcasted_iota(jnp.int32, gate.shape, 1) == expert
    return here, jnp.sum(jnp.where(here, gate, 0.0), axis=1, keepdims=True)


def decode(code, rows):
    wide_code = code.astype(jnp.float32)
    return (wide_code[:, :rows] + wide_code[:, rows:]).T


def far_kernel(plan, *refs):
    count, rows = plan
    refs = list(refs)
    take = lambda number: [refs.pop(0) for _ in range(number)]
    (first_ref,), pieces, weights_in = take(1), take(count), [take(2) for _ in range(4)]
    (act_out, hid_out), pieces_out = take(2), take(count)
    (tok, grad, coded_rows, extra), values = take(4), take(2)
    weights, stages, (sems_in, sems_out) = take(4), take(2), take(2)
    hidden = weights[0].shape[0] // 2
    tile = 2 * rows
    loads, stores = Copies(sems_in), Copies(sems_out)
    weight_ready, ready = [loads.pair(weights_in[0], weights[0])], []

    def load_tile(t):
        group = []
        for b in (2 * t, 2 * t + 1):
            at = pl.ds(b * rows, rows)
            group.append(loads.start(pieces[b].at[pl.ds(0, rows)], tok.at[at]))
            group.append(loads.start(pieces[b].at[pl.ds(rows, rows)], grad.at[at]))
            source = pieces[b].at[pl.ds(2 * rows, SPARE), pl.ds(0, 2 * rows)]
            group.append(loads.start(source, coded_rows.at[b]))
        ready.append(group)

    load_tile(0)
    for i in range(1, 4):
        weight_ready.append(loads.pair(weights_in[i], weights[i]))
    for t in range(1, count // 2):
        load_tile(t)
    first = first_ref[0]
    extra[...] = jnp.zeros_like(extra)
    staged, pending = [[], []], []
    for t in range(count // 2):
        span = pl.ds(t * tile, tile)
        for copy in ready[t]:
            copy.wait()
        gate = jnp.concatenate([decode(coded_rows[2 * t + k], rows) for k in range(2)], axis=0)
        total = 0.0
        for e in range(2):
            here, scale = gate_of(gate, first ^ e)
            part = 0.0
            for i in (2 * e, 2 * e + 1):
                if t == 0:
                    weight_ready[i].wait()
                part = part + hidden_part(
                    tok[span, :],
                    grad[span, :],
                    weights[i],
                    scale,
                    values[0].at[span],
                    values[1].at[span],
                    slice(i * hidden, (i + 1) * hidden),
                )
            total = total + jnp.where(here, part, 0.0)
        for value, target in zip(values, (act_out, hid_out)):
            source = value.at[span, pl.ds(0, 2 * hidden)]
            pending.append(stores.start(source, target.at[span]))
        for k in range(2):
            b = 2 * t + k
            encode(total[k * rows : (k + 1) * rows, :], extra, b, rows)
            pending.append(stores.start(extra.at[b], pieces_out[b].at[pl.ds(2 * rows, SPARE)]))
        for copy in staged[t % 2]:
            copy.wait()
        staged[t % 2] = []
        for kind, (stage, low) in enumerate(zip(stages, (hidden, 0))):
            lefts = [values[kind].at[span, pl.ds(i * hidden, hidden)] for i in range(4)]
            stage[t % 2] = partial_output(lefts, weights, low)
            for k in range(2):
                source = stage.at[t % 2, pl.ds(k * rows, rows)]
                target = pieces_out[2 * t + k].at[pl.ds(kind * rows, rows)]
                staged[t % 2].append(stores.start(source, target))
    for copy in pending + staged[0] + staged[1]:
        copy.wait()


def encode(score, extra, b, rows):
    rest = score.T
    high = rest.astype(jnp.bfloat16)
    extra[b, :, pl.ds(0, rows)] = high
    extra[b, :, pl.ds(rows, rows)] = (rest - high.astype(jnp.float32)).astype(jnp.bfloat16)


def partial_output(lefts, weights, low):
    hidden = weights[0].shape[0] // 2
    out = 0.0
    for left, weight in zip(lefts, weights):
        out = out + jnp.dot(
            left[...], weight[low : low + hidden, :], preferred_element_type=jnp.float32
        )
    return out.astype(jnp.bfloat16)


def split(stack, count, rows):
    step = 2 * rows + SPARE
    return [stack.at[pl.ds(b * step, step)] for b in range(count)]


def load_blocks(loads, blocks, slot, tok, grad, coded_rows, rows):
    started = []
    for k, block in enumerate(blocks):
        at = pl.ds(k * rows, rows)
        started.append(loads.start(block.at[pl.ds(0, rows)], tok.at[slot, at]))
        started.append(loads.start(block.at[pl.ds(rows, rows)], grad.at[slot, at]))
        if coded_rows is not None:
            source = block.at[pl.ds(2 * rows, SPARE), pl.ds(0, 2 * rows)]
            started.append(loads.start(source, coded_rows.at[slot, k]))
    return started


def add_sums(totals, acts, hids, tok, grad, slot, empty, results=None):
    hidden = totals.shape[1]
    for which, (left, right) in enumerate(((hids, tok), (acts, grad))):
        for k in range(2):
            out = contract_first(left[slot, :, k * hidden : (k + 1) * hidden], right[slot])
            if not empty:
                out = out + totals[2 * which + k]
            if results is None or k == 0:
                totals[2 * which + k] = out
            else:
                results[which] = out.astype(jnp.bfloat16)


def sums_kernel(plan, *refs):
    count, rows = plan
    refs = list(refs)
    take = lambda number: [refs.pop(0) for _ in range(number)]
    (first_ref,), near, far, (near_over,) = take(1), take(count), take(count), take(1)
    far_over, far_values = take(count), take(2)
    weights_in, near_values = [take(2) for _ in range(2)], take(2)
    keep_out, near_sums, (score,) = take(2), take(2), take(1)
    tok, grad, coded_rows, acts, hids, totals, results = take(7)
    weights, (sems_in, sems_out) = take(2), take(2)
    group = 4
    tile = group * rows
    hidden = weights[0].shape[0] // 2
    loads, stores = Copies(sems_in), Copies(sems_out)
    lists = [near, far, split(near_over, count, rows), far_over]
    steps = [
        (kind, g, blocks[g * group : (g + 1) * group])
        for kind, blocks in enumerate(lists)
        for g in range(count // group)
    ]

    def load(n):
        kind, g, blocks = steps[n]
        codes = None if kind == 1 else coded_rows
        started = load_blocks(loads, blocks, n % 2, tok, grad, codes, rows)
        if kind == 1:
            for source, target in zip(far_values, (acts, hids)):
                source = source.at[pl.ds(g * tile, tile)]
                started.append(loads.start(source, target.at[n % 2]))
        return started

    weight_ready = [loads.pair(weights_in[0], weights[0])]
    ready = load(0)
    weight_ready.append(loads.pair(weights_in[1], weights[1]))
    first = first_ref[0]
    saved = [[], []]
    for n, (kind, g, blocks) in enumerate(steps):
        slot = n % 2
        for copy in saved[1 - slot]:
            copy.wait()
        saved[1 - slot] = []
        coming = load(n + 1) if n + 1 < len(steps) else []
        for copy in ready:
            copy.wait()
        ready = coming
        if kind != 1:
            gate = jnp.concatenate([decode(coded_rows[slot, k], rows) for k in range(group)], axis=0)
            here, scale = gate_of(gate, first)
            part = 0.0
            for k in range(2):
                if n == 0:
                    weight_ready[k].wait()
                columns = slice(k * hidden, (k + 1) * hidden)
                part = part + hidden_part(
                    tok[slot], grad[slot], weights[k], scale, acts.at[slot], hids.at[slot], columns
                )
        if kind == 0:
            span = pl.ds(g * tile, tile)
            score[span, :] = jnp.where(here, part, 0.0)
            saved[slot] = [
                stores.start(acts.at[slot], near_values[0].at[span]),
                stores.start(hids.at[slot], near_values[1].at[span]),
            ]
        last = n + 1 == len(steps)
        add_sums(totals, acts, hids, tok, grad, slot, n == 0, results if last else None)
    tail = [stores.start(totals.at[2 * which], keep_out[which]) for which in range(2)]
    tail += [stores.start(results.at[which], near_sums[which]) for which in range(2)]
    for copy in saved[0] + saved[1] + tail:
        copy.wait()


def near_kernel(plan, *refs):
    count, rows = plan
    refs = list(refs)
    take = lambda number: [refs.pop(0) for _ in range(number)]
    (first_ref, score), near, values_in = take(2), take(count), take(2)
    weights_in = [take(2) for _ in range(4)]
    pieces_out = take(count)
    tok, grad, coded_rows, extra, acts, hids, others, outs = take(8)
    weights, (sems_in, sems_out) = take(4), take(2)
    hidden = weights[0].shape[0] // 2
    group = 4
    tile = group * rows
    loads, stores = Copies(sems_in), Copies(sems_out)

    def load(g):
        blocks, span = near[g * group : (g + 1) * group], pl.ds(g * tile, tile)
        started = load_blocks(loads, blocks, g % 2, tok, grad, coded_rows, rows)
        for source, target in zip(values_in, (acts, hids)):
            started.append(loads.start(source.at[span], target.at[g % 2]))
        return started

    weight_ready = {2: loads.pair(weights_in[2], weights[2])}
    ready = load(0)
    for i in (3, 0, 1):
        weight_ready[i] = loads.pair(weights_in[i], weights[i])
    first = first_ref[0]
    extra[...] = jnp.zeros_like(extra)
    out_copies = []
    for g in range(count // group):
        slot = g % 2
        coming = load(g + 1) if (g + 1) * group < count else []
        for copy in ready + out_copies:
            copy.wait()
        ready, out_copies = coming, []
        gate = jnp.concatenate([decode(coded_rows[slot, k], rows) for k in range(group)], axis=0)
        here, scale = gate_of(gate, first ^ 1)
        part = 0.0
        for k in range(2):
            if g == 0:
                weight_ready[2 + k].wait()
            columns = slice(k * hidden, (k + 1) * hidden)
            part = part + hidden_part(
                tok[slot], grad[slot], weights[2 + k], scale, others.at[0], others.at[1], columns
            )
        total = score[pl.ds(g * tile, tile), :] + jnp.where(here, part, 0.0)
        if g == 0:
            weight_ready[0].wait()
            weight_ready[1].wait()
        for k in range(group):
            b = g * group + k
            encode(total[k * rows : (k + 1) * rows, :], extra, b, rows)
            out_copies.append(stores.start(extra.at[b], pieces_out[b].at[pl.ds(2 * rows, SPARE)]))
        for which, (mine, low) in enumerate(((acts, hidden), (hids, 0))):
            lefts = [mine.at[slot, :, pl.ds(k * hidden, hidden)] for k in range(2)]
            lefts += [others.at[which, :, pl.ds(k * hidden, hidden)] for k in range(2)]
            outs[which] = partial_output(lefts, weights, low)
            for k in range(group):
                source = outs.at[which, pl.ds(k * rows, rows)]
                target = pieces_out[g * group + k].at[pl.ds(which * rows, rows)]
                out_copies.append(stores.start(source, target))
    for copy in out_copies:
        copy.wait()


ANYWHERE = pl.BlockSpec(memory_space=pl.ANY)
IN_VMEM = pl.BlockSpec(memory_space=pltpu.VMEM)
IN_SMEM = pl.BlockSpec(memory_space=pltpu.SMEM)
SPARE = 16


def kernel_params(flops=10**11):
    return dict(
        compiler_params=pltpu.CompilerParams(vmem_limit_bytes=58 * 2**20),
        cost_estimate=pl.CostEstimate(flops=flops, bytes_accessed=flops // 10**3, transcendentals=0),
    )


def far_call(rows, first, pieces, weights):
    count, features = len(pieces), pieces[0].shape[1]
    hidden = weights[0][0].shape[0]
    height = count * rows
    bf = jnp.bfloat16
    shape = jax.ShapeDtypeStruct
    outs = pl.pallas_call(
        functools.partial(far_kernel, (count, rows)),
        out_shape=[shape((height, 2 * hidden), bf)] * 2
        + [shape((2 * rows + SPARE, features), bf)] * count,
        in_specs=[IN_SMEM] + [ANYWHERE] * (count + 8),
        out_specs=[ANYWHERE] * (2 + count),
        scratch_shapes=[pltpu.VMEM((height, features), bf)] * 2
        + [pltpu.VMEM((count, SPARE, 2 * rows), bf)]
        + [pltpu.VMEM((count, SPARE, features), bf)]
        + [pltpu.VMEM((height, 4 * hidden), bf)] * 2
        + [pltpu.VMEM((2 * hidden, features), bf)] * 4
        + [pltpu.VMEM((2, 2 * rows, features), bf)] * 2
        + [pltpu.SemaphoreType.DMA((3 * count + 8,)), pltpu.SemaphoreType.DMA((4 * count,))],
        **kernel_params(),
    )(first, *pieces, *sum(weights, ()))
    return outs[:2], outs[2:]


def sums_call(rows, first, near, far, near_over, far_over, far_values, weights):
    count, features = len(near), near[0].shape[1]
    hidden = weights[0][0].shape[0]
    height, tile = count * rows, 4 * rows
    bf, f32 = jnp.bfloat16, jnp.float32
    shape = jax.ShapeDtypeStruct
    outs = pl.pallas_call(
        functools.partial(sums_kernel, (count, rows)),
        out_shape=[shape((height, 2 * hidden), bf)] * 2
        + [shape((hidden, features), f32)] * 2
        + [shape((hidden, features), bf)] * 2
        + [shape((height, SPARE), f32)],
        in_specs=[IN_SMEM] + [ANYWHERE] * (3 * count + 7),
        out_specs=[ANYWHERE] * 6 + [IN_VMEM],
        scratch_shapes=[pltpu.VMEM((2, tile, features), bf)] * 2
        + [pltpu.VMEM((2, 4, SPARE, 2 * rows), bf)]
        + [pltpu.VMEM((2, tile, 2 * hidden), bf)] * 2
        + [pltpu.VMEM((4, hidden, features), f32)]
        + [pltpu.VMEM((2, hidden, features), bf)]
        + [pltpu.VMEM((2 * hidden, features), bf)] * 2
        + [pltpu.SemaphoreType.DMA((12 * count + 4,)), pltpu.SemaphoreType.DMA((count + 4,))],
        **kernel_params(),
    )(first, *near, *far, near_over, *far_over, *far_values, *sum(weights, ()))
    return outs[:2], outs[2:4], outs[4:6], outs[6]


def near_call(rows, first, score, near, values, weights):
    count, features = len(near), near[0].shape[1]
    hidden = weights[0][0].shape[0]
    tile = 4 * rows
    bf = jnp.bfloat16
    return pl.pallas_call(
        functools.partial(near_kernel, (count, rows)),
        out_shape=[jax.ShapeDtypeStruct((2 * rows + SPARE, features), bf)] * count,
        in_specs=[IN_SMEM, IN_VMEM] + [ANYWHERE] * (count + 10),
        out_specs=[ANYWHERE] * count,
        scratch_shapes=[pltpu.VMEM((2, tile, features), bf)] * 2
        + [pltpu.VMEM((2, 4, SPARE, 2 * rows), bf)]
        + [pltpu.VMEM((count, SPARE, features), bf)]
        + [pltpu.VMEM((2, tile, 2 * hidden), bf)] * 3
        + [pltpu.VMEM((2, tile, features), bf)]
        + [pltpu.VMEM((2 * hidden, features), bf)] * 4
        + [pltpu.SemaphoreType.DMA((4 * count + 8,)), pltpu.SemaphoreType.DMA((3 * count,))],
        **kernel_params(1000),
    )(first, score, *near, *values, *sum(weights, ()))


def coded(rows_of, features):
    high = lax.reduce_precision(rows_of, 8, 7)
    both = jnp.concatenate([high, rows_of - high], axis=1).astype(jnp.bfloat16)
    return jnp.pad(both, ((0, SPARE - both.shape[0]), (0, features - both.shape[1])))


class Grid:
    def __init__(self, n_exp, n_fsdp):
        self.nx, self.ny = n_exp // CORES, n_fsdp // DEPTH

    def move(self, array, to):
        pairs = []
        for x in range(self.nx):
            for c in range(CORES):
                for z in range(DEPTH):
                    for y in range(self.ny):
                        tx, tc, tz, ty = to(x, c, z, y)
                        pairs.append((self.index(x, c, z, y), self.index(tx, tc, tz, ty)))
        return lax.ppermute(array, AXES, pairs)

    def index(self, x, c, z, y):
        return ((x * CORES + c) * DEPTH + z) * self.ny + y

    def spread(self, array, dx, dy):
        if dx == dy == 0:
            return array
        return self.move(
            array, lambda x, c, z, y: ((x - dx) % self.nx, c, z, (y - dy) % self.ny)
        )

    def collect(self, array, dx, dy):
        if dx == dy == 0:
            return array
        return self.move(
            array, lambda x, c, z, y: ((x + dx) % self.nx, c, z, (y + dy) % self.ny)
        )

    def swap_core(self, array):
        return self.move(array, lambda x, c, z, y: (x, 1 - c, z, y))

    def swap_far(self, array):
        return self.move(array, lambda x, c, z, y: (x, c, z ^ 2, y))

    def swap_near(self, array):
        return self.move(array, lambda x, c, z, y: (x, c, z ^ 1, y))


def wide(array):
    return array.astype(jnp.float32)


def total(parts):
    out = wide(parts[0])
    for part in parts[1:]:
        out = out + wide(part)
    return out


def tie(*groups):
    return lax.optimization_barrier(groups)


def shards(tokens, expert_ids, gates, w_in, w_out, grad_y):
    rows, features = tokens.shape
    n_exp, n_fsdp = lax.axis_size("exp"), lax.axis_size("fsdp")
    grid = Grid(n_exp, n_fsdp)
    steps = [(xo, yo) for yo in range(grid.ny) for xo in range(grid.nx)]
    bf = jnp.bfloat16
    first = jnp.reshape(lax.axis_index("exp"), (1,))

    ids_row = expert_ids.T[None, :, :]
    named = ids_row == jnp.arange(n_exp, dtype=jnp.int32)[:, None, None]
    gate_rows = jnp.sum(jnp.where(named, gates.T[None], 0.0), axis=1)

    own = jnp.concatenate([tokens, grad_y, coded(gate_rows, features)], axis=0)
    far = grid.swap_far(own)
    own_pair = (w_in[0], w_out[0])
    near_pieces = [grid.spread(own, *step) for step in steps]
    near_pieces, far, after_far = tie(near_pieces, far, own_pair)
    near_pair = tuple(grid.swap_near(part) for part in after_far)
    far_pieces = [grid.spread(far, *step) for step in steps]
    near_over = grid.swap_core(jnp.concatenate(near_pieces, axis=0))
    other_own = tuple(grid.swap_core(part) for part in own_pair)
    other_near = tuple(grid.swap_core(part) for part in near_pair)
    weights = [own_pair, near_pair, other_own, other_near]
    far_values, far_out = far_call(rows, first, far_pieces, weights)

    far_home = [grid.collect(part, *step) for part, step in zip(far_out, steps)]
    far_over = [grid.swap_core(piece) for piece in far_pieces]
    near_values, keep, near_sums, score = sums_call(
        rows, first, near_pieces, far_pieces, near_over, far_over, far_values, weights[:2]
    )
    near_out = near_call(rows, first, score, near_pieces, near_values, weights)
    far_home, near_out, _ = tie(far_home, near_out, near_sums)
    near_sums = [grid.swap_near(part) for part in near_sums]
    far_home = total(far_home)

    def score_of(home):
        return home[2 * rows :, :rows] + home[2 * rows :, rows : 2 * rows]

    far_home = jnp.concatenate(
        [far_home[: 2 * rows].astype(bf), coded(score_of(far_home), features)], axis=0
    )
    far_home = grid.swap_far(far_home)
    near_home = total([grid.collect(part, *step) for part, step in zip(near_out, steps)])

    home = near_home + wide(far_home)
    mixed, grad_tokens = home[:rows].astype(bf), home[rows : 2 * rows].astype(bf)
    score = score_of(home)[:n_exp]
    grad_gates = jnp.sum(jnp.where(named, score[:, None, :], 0.0), axis=0).T
    grad_in, grad_out = [mine + wide(theirs) for mine, theirs in zip(keep, near_sums)]
    return (mixed, grad_tokens, grad_in[None], grad_out[None], grad_gates)


def solution(mesh):
    rows = P(AXES, None)
    weights = P("exp", "fsdp", None)
    return jax.shard_map(
        shards,
        mesh=mesh,
        in_specs=(rows, rows, rows, weights, weights, rows),
        out_specs=(rows, rows, weights, weights, rows),
        check_vma=False,
    )
```

```python
import functools

import jax
import jax.numpy as jnp
from jax import lax
from jax.experimental import pallas as pl
from jax.experimental.pallas import tpu as pltpu
from jax.sharding import PartitionSpec as P

inv_sqrt_two = 0.7071067811865476
inv_sqrt_two_pi = 0.3989422804014327
AXES = ("exp", "fsdp")
CORES = 2
DEPTH = 4


def contract_first(left, right):
    return lax.dot_general(
        left, right, (((0,), (0,)), ((), ())), preferred_element_type=jnp.float32
    )


def contract_last(left, right):
    return lax.dot_general(
        left, right, (((1,), (1,)), ((), ())), preferred_element_type=jnp.float32
    )


def gelu_parts(values):
    cdf_part = 0.5 * (1.0 + lax.erf(values * inv_sqrt_two))
    return (
        values * cdf_part,
        cdf_part + values * jnp.exp(-0.5 * values * values) * inv_sqrt_two_pi,
    )


class Copies:
    def __init__(self, sems):
        self.sems, self.all = sems, []

    def start(self, source, target):
        copy = pltpu.make_async_copy(source, target, self.sems.at[len(self.all)])
        copy.start()
        self.all.append(copy)
        return copy

    def pair(self, sources, target):
        hidden = target.shape[0] // 2
        return Both(
            [self.start(sources[k], target.at[pl.ds(k * hidden, hidden)]) for k in range(2)]
        )


class Both:
    def __init__(self, copies):
        self.copies = copies

    def wait(self):
        for copy in self.copies:
            copy.wait()


def hidden_part(tok, grad, weight, scale, act_ref, hid_ref, columns):
    hidden = weight.shape[0] // 2
    pre = contract_last(tok, weight[:hidden, :])
    back = contract_last(grad, weight[hidden:, :])
    full, slope = gelu_parts(pre)
    act_ref[:, columns] = (full * scale).astype(jnp.bfloat16)
    hid_ref[:, columns] = (back * slope * scale).astype(jnp.bfloat16)
    return jnp.sum(full * back, axis=1, keepdims=True)


def gate_of(gate, expert):
    here = lax.broadcasted_iota(jnp.int32, gate.shape, 1) == expert
    return here, jnp.sum(jnp.where(here, gate, 0.0), axis=1, keepdims=True)


def decode(code, rows):
    wide_code = code.astype(jnp.float32)
    return (wide_code[:, :rows] + wide_code[:, rows:]).T


def far_kernel(plan, *refs):
    count, rows = plan
    refs = list(refs)
    take = lambda number: [refs.pop(0) for _ in range(number)]
    (first_ref,), pieces, weights_in = take(1), take(count), [take(2) for _ in range(4)]
    (act_out, hid_out), pieces_out = take(2), take(count)
    (tok, grad, coded_rows, extra), values = take(4), take(2)
    weights, stages, (sems_in, sems_out) = take(4), take(2), take(2)
    hidden = weights[0].shape[0] // 2
    tile = 2 * rows
    loads, stores = Copies(sems_in), Copies(sems_out)
    weight_ready, ready = [loads.pair(weights_in[0], weights[0])], []

    def load_tile(t):
        group = []
        for b in (2 * t, 2 * t + 1):
            at = pl.ds(b * rows, rows)
            group.append(loads.start(pieces[b].at[pl.ds(0, rows)], tok.at[at]))
            group.append(loads.start(pieces[b].at[pl.ds(rows, rows)], grad.at[at]))
            source = pieces[b].at[pl.ds(2 * rows, SPARE), pl.ds(0, 2 * rows)]
            group.append(loads.start(source, coded_rows.at[b]))
        ready.append(group)

    load_tile(0)
    for i in range(1, 4):
        weight_ready.append(loads.pair(weights_in[i], weights[i]))
    for t in range(1, count // 2):
        load_tile(t)
    first = first_ref[0]
    extra[...] = jnp.zeros_like(extra)
    staged, pending = [[], []], []
    for t in range(count // 2):
        span = pl.ds(t * tile, tile)
        for copy in ready[t]:
            copy.wait()
        gate = jnp.concatenate([decode(coded_rows[2 * t + k], rows) for k in range(2)], axis=0)
        total = 0.0
        for e in range(2):
            here, scale = gate_of(gate, first ^ e)
            part = 0.0
            for i in (2 * e, 2 * e + 1):
                if t == 0:
                    weight_ready[i].wait()
                part = part + hidden_part(
                    tok[span, :],
                    grad[span, :],
                    weights[i],
                    scale,
                    values[0].at[span],
                    values[1].at[span],
                    slice(i * hidden, (i + 1) * hidden),
                )
            total = total + jnp.where(here, part, 0.0)
        for value, target in zip(values, (act_out, hid_out)):
            source = value.at[span, pl.ds(0, 2 * hidden)]
            pending.append(stores.start(source, target.at[span]))
        for k in range(2):
            b = 2 * t + k
            encode(total[k * rows : (k + 1) * rows, :], extra, b, rows)
            pending.append(stores.start(extra.at[b], pieces_out[b].at[pl.ds(2 * rows, SPARE)]))
        for copy in staged[t % 2]:
            copy.wait()
        staged[t % 2] = []
        for kind, (stage, low) in enumerate(zip(stages, (hidden, 0))):
            lefts = [values[kind].at[span, pl.ds(i * hidden, hidden)] for i in range(4)]
            stage[t % 2] = partial_output(lefts, weights, low)
            for k in range(2):
                source = stage.at[t % 2, pl.ds(k * rows, rows)]
                target = pieces_out[2 * t + k].at[pl.ds(kind * rows, rows)]
                staged[t % 2].append(stores.start(source, target))
    for copy in pending + staged[0] + staged[1]:
        copy.wait()


def encode(score, extra, b, rows):
    rest = score.T
    high = rest.astype(jnp.bfloat16)
    extra[b, :, pl.ds(0, rows)] = high
    extra[b, :, pl.ds(rows, rows)] = (rest - high.astype(jnp.float32)).astype(jnp.bfloat16)


def partial_output(lefts, weights, low):
    hidden = weights[0].shape[0] // 2
    out = 0.0
    for left, weight in zip(lefts, weights):
        out = out + jnp.dot(
            left[...], weight[low : low + hidden, :], preferred_element_type=jnp.float32
        )
    return out.astype(jnp.bfloat16)


def split(stack, count, rows):
    step = 2 * rows + SPARE
    return [stack.at[pl.ds(b * step, step)] for b in range(count)]


def load_blocks(loads, blocks, slot, tok, grad, coded_rows, rows):
    started = []
    for k, block in enumerate(blocks):
        at = pl.ds(k * rows, rows)
        started.append(loads.start(block.at[pl.ds(0, rows)], tok.at[slot, at]))
        started.append(loads.start(block.at[pl.ds(rows, rows)], grad.at[slot, at]))
        if coded_rows is not None:
            source = block.at[pl.ds(2 * rows, SPARE), pl.ds(0, 2 * rows)]
            started.append(loads.start(source, coded_rows.at[slot, k]))
    return started


def add_sums(totals, acts, hids, tok, grad, slot, empty, results=None):
    hidden = totals.shape[1]
    for which, (left, right) in enumerate(((hids, tok), (acts, grad))):
        for k in range(2):
            out = contract_first(left[slot, :, k * hidden : (k + 1) * hidden], right[slot])
            if not empty:
                out = out + totals[2 * which + k]
            if results is None or k == 0:
                totals[2 * which + k] = out
            else:
                results[which] = out.astype(jnp.bfloat16)


def sums_kernel(plan, *refs):
    count, rows = plan
    refs = list(refs)
    take = lambda number: [refs.pop(0) for _ in range(number)]
    (first_ref,), near, far, (near_over,) = take(1), take(count), take(count), take(1)
    far_over, far_values = take(count), take(2)
    weights_in, near_values = [take(2) for _ in range(2)], take(2)
    keep_out, near_sums, (score,) = take(2), take(2), take(1)
    tok, grad, coded_rows, acts, hids, totals, results = take(7)
    weights, (sems_in, sems_out) = take(2), take(2)
    group = 4
    tile = group * rows
    hidden = weights[0].shape[0] // 2
    loads, stores = Copies(sems_in), Copies(sems_out)
    lists = [near, far, split(near_over, count, rows), far_over]
    steps = [
        (kind, g, blocks[g * group : (g + 1) * group])
        for kind, blocks in enumerate(lists)
        for g in range(count // group)
    ]

    def load(n):
        kind, g, blocks = steps[n]
        codes = None if kind == 1 else coded_rows
        started = load_blocks(loads, blocks, n % 2, tok, grad, codes, rows)
        if kind == 1:
            for source, target in zip(far_values, (acts, hids)):
                source = source.at[pl.ds(g * tile, tile)]
                started.append(loads.start(source, target.at[n % 2]))
        return started

    weight_ready = [loads.pair(weights_in[0], weights[0])]
    ready = load(0)
    weight_ready.append(loads.pair(weights_in[1], weights[1]))
    first = first_ref[0]
    saved = [[], []]
    for n, (kind, g, blocks) in enumerate(steps):
        slot = n % 2
        for copy in saved[1 - slot]:
            copy.wait()
        saved[1 - slot] = []
        coming = load(n + 1) if n + 1 < len(steps) else []
        for copy in ready:
            copy.wait()
        ready = coming
        if kind != 1:
            gate = jnp.concatenate([decode(coded_rows[slot, k], rows) for k in range(group)], axis=0)
            here, scale = gate_of(gate, first)
            part = 0.0
            for k in range(2):
                if n == 0:
                    weight_ready[k].wait()
                columns = slice(k * hidden, (k + 1) * hidden)
                part = part + hidden_part(
                    tok[slot], grad[slot], weights[k], scale, acts.at[slot], hids.at[slot], columns
                )
        if kind == 0:
            span = pl.ds(g * tile, tile)
            score[span, :] = jnp.where(here, part, 0.0)
            saved[slot] = [
                stores.start(acts.at[slot], near_values[0].at[span]),
                stores.start(hids.at[slot], near_values[1].at[span]),
            ]
        last = n + 1 == len(steps)
        add_sums(totals, acts, hids, tok, grad, slot, n == 0, results if last else None)
    tail = [stores.start(totals.at[2 * which], keep_out[which]) for which in range(2)]
    tail += [stores.start(results.at[which], near_sums[which]) for which in range(2)]
    for copy in saved[0] + saved[1] + tail:
        copy.wait()


def near_kernel(plan, *refs):
    count, rows = plan
    refs = list(refs)
    take = lambda number: [refs.pop(0) for _ in range(number)]
    (first_ref, score), near, values_in = take(2), take(count), take(2)
    weights_in = [take(2) for _ in range(4)]
    pieces_out = take(count)
    tok, grad, coded_rows, extra, acts, hids, others, outs = take(8)
    weights, (sems_in, sems_out) = take(4), take(2)
    hidden = weights[0].shape[0] // 2
    group = 4
    tile = group * rows
    loads, stores = Copies(sems_in), Copies(sems_out)

    def load(g):
        blocks, span = near[g * group : (g + 1) * group], pl.ds(g * tile, tile)
        started = load_blocks(loads, blocks, g % 2, tok, grad, coded_rows, rows)
        for source, target in zip(values_in, (acts, hids)):
            started.append(loads.start(source.at[span], target.at[g % 2]))
        return started

    weight_ready = {2: loads.pair(weights_in[2], weights[2])}
    ready = load(0)
    for i in (3, 0, 1):
        weight_ready[i] = loads.pair(weights_in[i], weights[i])
    first = first_ref[0]
    extra[...] = jnp.zeros_like(extra)
    out_copies = []
    for g in range(count // group):
        slot = g % 2
        coming = load(g + 1) if (g + 1) * group < count else []
        for copy in ready + out_copies:
            copy.wait()
        ready, out_copies = coming, []
        gate = jnp.concatenate([decode(coded_rows[slot, k], rows) for k in range(group)], axis=0)
        here, scale = gate_of(gate, first ^ 1)
        part = 0.0
        for k in range(2):
            if g == 0:
                weight_ready[2 + k].wait()
            columns = slice(k * hidden, (k + 1) * hidden)
            part = part + hidden_part(
                tok[slot], grad[slot], weights[2 + k], scale, others.at[0], others.at[1], columns
            )
        total = score[pl.ds(g * tile, tile), :] + jnp.where(here, part, 0.0)
        if g == 0:
            weight_ready[0].wait()
            weight_ready[1].wait()
        for k in range(group):
            b = g * group + k
            encode(total[k * rows : (k + 1) * rows, :], extra, b, rows)
            out_copies.append(stores.start(extra.at[b], pieces_out[b].at[pl.ds(2 * rows, SPARE)]))
        for which, (mine, low) in enumerate(((acts, hidden), (hids, 0))):
            lefts = [mine.at[slot, :, pl.ds(k * hidden, hidden)] for k in range(2)]
            lefts += [others.at[which, :, pl.ds(k * hidden, hidden)] for k in range(2)]
            outs[which] = partial_output(lefts, weights, low)
            for k in range(group):
                source = outs.at[which, pl.ds(k * rows, rows)]
                target = pieces_out[g * group + k].at[pl.ds(which * rows, rows)]
                out_copies.append(stores.start(source, target))
    for copy in out_copies:
        copy.wait()


ANYWHERE = pl.BlockSpec(memory_space=pl.ANY)
IN_VMEM = pl.BlockSpec(memory_space=pltpu.VMEM)
IN_SMEM = pl.BlockSpec(memory_space=pltpu.SMEM)
SPARE = 16


def kernel_params(flops=10**11):
    return dict(
        compiler_params=pltpu.CompilerParams(vmem_limit_bytes=58 * 2**20),
        cost_estimate=pl.CostEstimate(flops=flops, bytes_accessed=flops // 10**3, transcendentals=0),
    )


def far_call(rows, first, pieces, weights):
    count, features = len(pieces), pieces[0].shape[1]
    hidden = weights[0][0].shape[0]
    height = count * rows
    bf = jnp.bfloat16
    shape = jax.ShapeDtypeStruct
    outs = pl.pallas_call(
        functools.partial(far_kernel, (count, rows)),
        out_shape=[shape((height, 2 * hidden), bf)] * 2
        + [shape((2 * rows + SPARE, features), bf)] * count,
        in_specs=[IN_SMEM] + [ANYWHERE] * (count + 8),
        out_specs=[ANYWHERE] * (2 + count),
        scratch_shapes=[pltpu.VMEM((height, features), bf)] * 2
        + [pltpu.VMEM((count, SPARE, 2 * rows), bf)]
        + [pltpu.VMEM((count, SPARE, features), bf)]
        + [pltpu.VMEM((height, 4 * hidden), bf)] * 2
        + [pltpu.VMEM((2 * hidden, features), bf)] * 4
        + [pltpu.VMEM((2, 2 * rows, features), bf)] * 2
        + [pltpu.SemaphoreType.DMA((3 * count + 8,)), pltpu.SemaphoreType.DMA((4 * count,))],
        **kernel_params(),
    )(first, *pieces, *sum(weights, ()))
    return outs[:2], outs[2:]


def sums_call(rows, first, near, far, near_over, far_over, far_values, weights):
    count, features = len(near), near[0].shape[1]
    hidden = weights[0][0].shape[0]
    height, tile = count * rows, 4 * rows
    bf, f32 = jnp.bfloat16, jnp.float32
    shape = jax.ShapeDtypeStruct
    outs = pl.pallas_call(
        functools.partial(sums_kernel, (count, rows)),
        out_shape=[shape((height, 2 * hidden), bf)] * 2
        + [shape((hidden, features), f32)] * 2
        + [shape((hidden, features), bf)] * 2
        + [shape((height, SPARE), f32)],
        in_specs=[IN_SMEM] + [ANYWHERE] * (3 * count + 7),
        out_specs=[ANYWHERE] * 6 + [IN_VMEM],
        scratch_shapes=[pltpu.VMEM((2, tile, features), bf)] * 2
        + [pltpu.VMEM((2, 4, SPARE, 2 * rows), bf)]
        + [pltpu.VMEM((2, tile, 2 * hidden), bf)] * 2
        + [pltpu.VMEM((4, hidden, features), f32)]
        + [pltpu.VMEM((2, hidden, features), bf)]
        + [pltpu.VMEM((2 * hidden, features), bf)] * 2
        + [pltpu.SemaphoreType.DMA((12 * count + 4,)), pltpu.SemaphoreType.DMA((count + 4,))],
        **kernel_params(),
    )(first, *near, *far, near_over, *far_over, *far_values, *sum(weights, ()))
    return outs[:2], outs[2:4], outs[4:6], outs[6]


def near_call(rows, first, score, near, values, weights):
    count, features = len(near), near[0].shape[1]
    hidden = weights[0][0].shape[0]
    tile = 4 * rows
    bf = jnp.bfloat16
    return pl.pallas_call(
        functools.partial(near_kernel, (count, rows)),
        out_shape=[jax.ShapeDtypeStruct((2 * rows + SPARE, features), bf)] * count,
        in_specs=[IN_SMEM, IN_VMEM] + [ANYWHERE] * (count + 10),
        out_specs=[ANYWHERE] * count,
        scratch_shapes=[pltpu.VMEM((2, tile, features), bf)] * 2
        + [pltpu.VMEM((2, 4, SPARE, 2 * rows), bf)]
        + [pltpu.VMEM((count, SPARE, features), bf)]
        + [pltpu.VMEM((2, tile, 2 * hidden), bf)] * 3
        + [pltpu.VMEM((2, tile, features), bf)]
        + [pltpu.VMEM((2 * hidden, features), bf)] * 4
        + [pltpu.SemaphoreType.DMA((4 * count + 8,)), pltpu.SemaphoreType.DMA((3 * count,))],
        **kernel_params(1000),
    )(first, score, *near, *values, *sum(weights, ()))


def coded(rows_of, features):
    high = lax.reduce_precision(rows_of, 8, 7)
    both = jnp.concatenate([high, rows_of - high], axis=1).astype(jnp.bfloat16)
    return jnp.pad(both, ((0, SPARE - both.shape[0]), (0, features - both.shape[1])))


class Grid:
    def __init__(self, n_exp, n_fsdp):
        self.nx, self.ny = n_exp // CORES, n_fsdp // DEPTH

    def move(self, array, to):
        pairs = []
        for x in range(self.nx):
            for c in range(CORES):
                for z in range(DEPTH):
                    for y in range(self.ny):
                        tx, tc, tz, ty = to(x, c, z, y)
                        pairs.append((self.index(x, c, z, y), self.index(tx, tc, tz, ty)))
        return lax.ppermute(array, AXES, pairs)

    def index(self, x, c, z, y):
        return ((x * CORES + c) * DEPTH + z) * self.ny + y

    def spread(self, array, dx, dy):
        if dx == dy == 0:
            return array
        return self.move(
            array, lambda x, c, z, y: ((x - dx) % self.nx, c, z, (y - dy) % self.ny)
        )

    def collect(self, array, dx, dy):
        if dx == dy == 0:
            return array
        return self.move(
            array, lambda x, c, z, y: ((x + dx) % self.nx, c, z, (y + dy) % self.ny)
        )

    def swap_core(self, array):
        return self.move(array, lambda x, c, z, y: (x, 1 - c, z, y))

    def swap_far(self, array):
        return self.move(array, lambda x, c, z, y: (x, c, z ^ 2, y))

    def swap_near(self, array):
        return self.move(array, lambda x, c, z, y: (x, c, z ^ 1, y))


def wide(array):
    return array.astype(jnp.float32)


def total(parts):
    out = wide(parts[0])
    for part in parts[1:]:
        out = out + wide(part)
    return out


def tie(*groups):
    return lax.optimization_barrier(groups)


def shards(tokens, expert_ids, gates, w_in, w_out, grad_y):
    rows, features = tokens.shape
    n_exp, n_fsdp = lax.axis_size("exp"), lax.axis_size("fsdp")
    grid = Grid(n_exp, n_fsdp)
    steps = [(xo, yo) for yo in range(grid.ny) for xo in range(grid.nx)]
    bf = jnp.bfloat16
    first = jnp.reshape(lax.axis_index("exp"), (1,))

    ids_row = expert_ids.T[None, :, :]
    named = ids_row == jnp.arange(n_exp, dtype=jnp.int32)[:, None, None]
    gate_rows = jnp.sum(jnp.where(named, gates.T[None], 0.0), axis=1)

    own = jnp.concatenate([tokens, grad_y, coded(gate_rows, features)], axis=0)
    far = grid.swap_far(own)
    own_pair = (w_in[0], w_out[0])
    near_pieces = [grid.spread(own, *step) for step in steps]
    near_pieces, far = tie(near_pieces, far)
    near_pair = tuple(grid.swap_near(part) for part in own_pair)
    far_pieces = [grid.spread(far, *step) for step in steps]
    near_over = grid.swap_core(jnp.concatenate(near_pieces, axis=0))
    other_own = tuple(grid.swap_core(part) for part in own_pair)
    other_near = tuple(grid.swap_core(part) for part in near_pair)
    weights = [own_pair, near_pair, other_own, other_near]
    far_values, far_out = far_call(rows, first, far_pieces, weights)

    far_home = [grid.collect(part, *step) for part, step in zip(far_out, steps)]
    far_over = [grid.swap_core(piece) for piece in far_pieces]
    near_values, keep, near_sums, score = sums_call(
        rows, first, near_pieces, far_pieces, near_over, far_over, far_values, weights[:2]
    )
    near_out = near_call(rows, first, score, near_pieces, near_values, weights)
    far_home, near_out, _ = tie(far_home, near_out, near_sums)
    near_sums = [grid.swap_near(part) for part in near_sums]
    far_home = total(far_home)

    def score_of(home):
        return home[2 * rows :, :rows] + home[2 * rows :, rows : 2 * rows]

    far_home = jnp.concatenate(
        [far_home[: 2 * rows].astype(bf), coded(score_of(far_home), features)], axis=0
    )
    far_home = grid.swap_far(far_home)
    near_home = total([grid.collect(part, *step) for part, step in zip(near_out, steps)])

    home = near_home + wide(far_home)
    mixed, grad_tokens = home[:rows].astype(bf), home[rows : 2 * rows].astype(bf)
    score = score_of(home)[:n_exp]
    grad_gates = jnp.sum(jnp.where(named, score[:, None, :], 0.0), axis=0).T
    grad_in, grad_out = [mine + wide(theirs) for mine, theirs in zip(keep, near_sums)]
    return (mixed, grad_tokens, grad_in[None], grad_out[None], grad_gates)


def solution(mesh):
    rows = P(AXES, None)
    weights = P("exp", "fsdp", None)
    return jax.shard_map(
        shards,
        mesh=mesh,
        in_specs=(rows, rows, rows, weights, weights, rows),
        out_specs=(rows, rows, weights, weights, rows),
        check_vma=False,
    )
```

```python
import functools

import jax
import jax.numpy as jnp
from jax import lax
from jax.experimental import pallas as pl
from jax.experimental.pallas import tpu as pltpu
from jax.sharding import PartitionSpec as P

inv_sqrt_two = 0.7071067811865476
inv_sqrt_two_pi = 0.3989422804014327
AXES = ("exp", "fsdp")
CORES = 2
DEPTH = 4


def contract_first(left, right):
    return lax.dot_general(
        left, right, (((0,), (0,)), ((), ())), preferred_element_type=jnp.float32
    )


def contract_last(left, right):
    return lax.dot_general(
        left, right, (((1,), (1,)), ((), ())), preferred_element_type=jnp.float32
    )


def gelu_parts(values):
    cdf_part = 0.5 * (1.0 + lax.erf(values * inv_sqrt_two))
    return (
        values * cdf_part,
        cdf_part + values * jnp.exp(-0.5 * values * values) * inv_sqrt_two_pi,
    )


class Copies:
    def __init__(self, sems):
        self.sems, self.all = sems, []

    def start(self, source, target):
        copy = pltpu.make_async_copy(source, target, self.sems.at[len(self.all)])
        copy.start()
        self.all.append(copy)
        return copy

    def pair(self, sources, target):
        hidden = target.shape[0] // 2
        return Both(
            [self.start(sources[k], target.at[pl.ds(k * hidden, hidden)]) for k in range(2)]
        )


class Both:
    def __init__(self, copies):
        self.copies = copies

    def wait(self):
        for copy in self.copies:
            copy.wait()


def hidden_part(tok, grad, weight, scale, act_ref, hid_ref, columns):
    hidden = weight.shape[0] // 2
    pre = contract_last(tok, weight[:hidden, :])
    back = contract_last(grad, weight[hidden:, :])
    full, slope = gelu_parts(pre)
    act_ref[:, columns] = (full * scale).astype(jnp.bfloat16)
    hid_ref[:, columns] = (back * slope * scale).astype(jnp.bfloat16)
    return jnp.sum(full * back, axis=1, keepdims=True)


def gate_of(gate, expert):
    here = lax.broadcasted_iota(jnp.int32, gate.shape, 1) == expert
    return here, jnp.sum(jnp.where(here, gate, 0.0), axis=1, keepdims=True)


def decode(code, rows):
    wide_code = code.astype(jnp.float32)
    return (wide_code[:, :rows] + wide_code[:, rows:]).T


def far_kernel(plan, *refs):
    count, rows = plan
    refs = list(refs)
    take = lambda number: [refs.pop(0) for _ in range(number)]
    (first_ref,), pieces, weights_in = take(1), take(count), [take(2) for _ in range(4)]
    (act_out, hid_out), pieces_out = take(2), take(count)
    (tok, grad, coded_rows, extra), values = take(4), take(2)
    weights, stages, (sems_in, sems_out) = take(4), take(2), take(2)
    hidden = weights[0].shape[0] // 2
    tile = 2 * rows
    loads, stores = Copies(sems_in), Copies(sems_out)
    weight_ready, ready = [loads.pair(weights_in[0], weights[0])], []

    def load_tile(t):
        group = []
        for b in (2 * t, 2 * t + 1):
            at = pl.ds(b * rows, rows)
            group.append(loads.start(pieces[b].at[pl.ds(0, rows)], tok.at[at]))
            group.append(loads.start(pieces[b].at[pl.ds(rows, rows)], grad.at[at]))
            source = pieces[b].at[pl.ds(2 * rows, SPARE), pl.ds(0, 2 * rows)]
            group.append(loads.start(source, coded_rows.at[b]))
        ready.append(group)

    load_tile(0)
    for i in range(1, 4):
        weight_ready.append(loads.pair(weights_in[i], weights[i]))
    for t in range(1, count // 2):
        load_tile(t)
    first = first_ref[0]
    extra[...] = jnp.zeros_like(extra)
    staged, pending = [[], []], []
    for t in range(count // 2):
        span = pl.ds(t * tile, tile)
        for copy in ready[t]:
            copy.wait()
        gate = jnp.concatenate([decode(coded_rows[2 * t + k], rows) for k in range(2)], axis=0)
        total = 0.0
        for e in range(2):
            here, scale = gate_of(gate, first ^ e)
            part = 0.0
            for i in (2 * e, 2 * e + 1):
                if t == 0:
                    weight_ready[i].wait()
                part = part + hidden_part(
                    tok[span, :],
                    grad[span, :],
                    weights[i],
                    scale,
                    values[0].at[span],
                    values[1].at[span],
                    slice(i * hidden, (i + 1) * hidden),
                )
            total = total + jnp.where(here, part, 0.0)
        for value, target in zip(values, (act_out, hid_out)):
            source = value.at[span, pl.ds(0, 2 * hidden)]
            pending.append(stores.start(source, target.at[span]))
        for k in range(2):
            b = 2 * t + k
            encode(total[k * rows : (k + 1) * rows, :], extra, b, rows)
            pending.append(stores.start(extra.at[b], pieces_out[b].at[pl.ds(2 * rows, SPARE)]))
        for copy in staged[t % 2]:
            copy.wait()
        staged[t % 2] = []
        for kind, (stage, low) in enumerate(zip(stages, (hidden, 0))):
            lefts = [values[kind].at[span, pl.ds(i * hidden, hidden)] for i in range(4)]
            stage[t % 2] = partial_output(lefts, weights, low)
            for k in range(2):
                source = stage.at[t % 2, pl.ds(k * rows, rows)]
                target = pieces_out[2 * t + k].at[pl.ds(kind * rows, rows)]
                staged[t % 2].append(stores.start(source, target))
    for copy in pending + staged[0] + staged[1]:
        copy.wait()


def encode(score, extra, b, rows):
    rest = score.T
    high = rest.astype(jnp.bfloat16)
    extra[b, :, pl.ds(0, rows)] = high
    extra[b, :, pl.ds(rows, rows)] = (rest - high.astype(jnp.float32)).astype(jnp.bfloat16)


def partial_output(lefts, weights, low):
    hidden = weights[0].shape[0] // 2
    out = 0.0
    for left, weight in zip(lefts, weights):
        out = out + jnp.dot(
            left[...], weight[low : low + hidden, :], preferred_element_type=jnp.float32
        )
    return out.astype(jnp.bfloat16)


def split(stack, count, rows):
    step = 2 * rows + SPARE
    return [stack.at[pl.ds(b * step, step)] for b in range(count)]


def load_blocks(loads, blocks, slot, tok, grad, coded_rows, rows):
    started = []
    for k, block in enumerate(blocks):
        at = pl.ds(k * rows, rows)
        started.append(loads.start(block.at[pl.ds(0, rows)], tok.at[slot, at]))
        started.append(loads.start(block.at[pl.ds(rows, rows)], grad.at[slot, at]))
        if coded_rows is not None:
            source = block.at[pl.ds(2 * rows, SPARE), pl.ds(0, 2 * rows)]
            started.append(loads.start(source, coded_rows.at[slot, k]))
    return started


def add_sums(totals, acts, hids, tok, grad, slot, empty, results=None):
    hidden = totals.shape[1]
    for which, (left, right) in enumerate(((hids, tok), (acts, grad))):
        for k in range(2):
            out = contract_first(left[slot, :, k * hidden : (k + 1) * hidden], right[slot])
            if not empty:
                out = out + totals[2 * which + k]
            if results is None or k == 0:
                totals[2 * which + k] = out
            else:
                results[which] = out.astype(jnp.bfloat16)


def sums_kernel(plan, *refs):
    count, rows = plan
    refs = list(refs)
    take = lambda number: [refs.pop(0) for _ in range(number)]
    (first_ref,), near, far, (near_over,) = take(1), take(count), take(count), take(1)
    far_over, far_values = take(count), take(2)
    weights_in, near_values = [take(2) for _ in range(2)], take(2)
    keep_out, near_sums, (score,) = take(2), take(2), take(1)
    tok, grad, coded_rows, acts, hids, totals, results = take(7)
    weights, (sems_in, sems_out) = take(2), take(2)
    group = 4
    tile = group * rows
    hidden = weights[0].shape[0] // 2
    loads, stores = Copies(sems_in), Copies(sems_out)
    lists = [near, far, split(near_over, count, rows), far_over]
    steps = [
        (kind, g, blocks[g * group : (g + 1) * group])
        for kind, blocks in enumerate(lists)
        for g in range(count // group)
    ]

    def load(n):
        kind, g, blocks = steps[n]
        codes = None if kind == 1 else coded_rows
        started = load_blocks(loads, blocks, n % 2, tok, grad, codes, rows)
        if kind == 1:
            for source, target in zip(far_values, (acts, hids)):
                source = source.at[pl.ds(g * tile, tile)]
                started.append(loads.start(source, target.at[n % 2]))
        return started

    weight_ready = [loads.pair(weights_in[0], weights[0])]
    ready = load(0)
    weight_ready.append(loads.pair(weights_in[1], weights[1]))
    first = first_ref[0]
    saved = [[], []]
    for n, (kind, g, blocks) in enumerate(steps):
        slot = n % 2
        for copy in saved[1 - slot]:
            copy.wait()
        saved[1 - slot] = []
        coming = load(n + 1) if n + 1 < len(steps) else []
        for copy in ready:
            copy.wait()
        ready = coming
        if kind != 1:
            gate = jnp.concatenate([decode(coded_rows[slot, k], rows) for k in range(group)], axis=0)
            here, scale = gate_of(gate, first)
            part = 0.0
            for k in range(2):
                if n == 0:
                    weight_ready[k].wait()
                columns = slice(k * hidden, (k + 1) * hidden)
                part = part + hidden_part(
                    tok[slot], grad[slot], weights[k], scale, acts.at[slot], hids.at[slot], columns
                )
        if kind == 0:
            span = pl.ds(g * tile, tile)
            score[span, :] = jnp.where(here, part, 0.0)
            saved[slot] = [
                stores.start(acts.at[slot], near_values[0].at[span]),
                stores.start(hids.at[slot], near_values[1].at[span]),
            ]
        last = n + 1 == len(steps)
        add_sums(totals, acts, hids, tok, grad, slot, n == 0, results if last else None)
    tail = [stores.start(totals.at[2 * which], keep_out[which]) for which in range(2)]
    tail += [stores.start(results.at[which], near_sums[which]) for which in range(2)]
    for copy in saved[0] + saved[1] + tail:
        copy.wait()


def near_kernel(plan, *refs):
    count, rows = plan
    refs = list(refs)
    take = lambda number: [refs.pop(0) for _ in range(number)]
    (first_ref, score), near, values_in = take(2), take(count), take(2)
    weights_in = [take(2) for _ in range(4)]
    pieces_out = take(count)
    tok, grad, coded_rows, extra, acts, hids, others, outs = take(8)
    weights, (sems_in, sems_out) = take(4), take(2)
    hidden = weights[0].shape[0] // 2
    group = 4
    tile = group * rows
    loads, stores = Copies(sems_in), Copies(sems_out)

    def load(g):
        blocks, span = near[g * group : (g + 1) * group], pl.ds(g * tile, tile)
        started = load_blocks(loads, blocks, g % 2, tok, grad, coded_rows, rows)
        for source, target in zip(values_in, (acts, hids)):
            started.append(loads.start(source.at[span], target.at[g % 2]))
        return started

    weight_ready = {2: loads.pair(weights_in[2], weights[2])}
    ready = load(0)
    for i in (3, 0, 1):
        weight_ready[i] = loads.pair(weights_in[i], weights[i])
    first = first_ref[0]
    extra[...] = jnp.zeros_like(extra)
    out_copies = []
    for g in range(count // group):
        slot = g % 2
        coming = load(g + 1) if (g + 1) * group < count else []
        for copy in ready + out_copies:
            copy.wait()
        ready, out_copies = coming, []
        gate = jnp.concatenate([decode(coded_rows[slot, k], rows) for k in range(group)], axis=0)
        here, scale = gate_of(gate, first ^ 1)
        part = 0.0
        for k in range(2):
            if g == 0:
                weight_ready[2 + k].wait()
            columns = slice(k * hidden, (k + 1) * hidden)
            part = part + hidden_part(
                tok[slot], grad[slot], weights[2 + k], scale, others.at[0], others.at[1], columns
            )
        total = score[pl.ds(g * tile, tile), :] + jnp.where(here, part, 0.0)
        if g == 0:
            weight_ready[0].wait()
            weight_ready[1].wait()
        for k in range(group):
            b = g * group + k
            encode(total[k * rows : (k + 1) * rows, :], extra, b, rows)
            out_copies.append(stores.start(extra.at[b], pieces_out[b].at[pl.ds(2 * rows, SPARE)]))
        for which, (mine, low) in enumerate(((acts, hidden), (hids, 0))):
            lefts = [mine.at[slot, :, pl.ds(k * hidden, hidden)] for k in range(2)]
            lefts += [others.at[which, :, pl.ds(k * hidden, hidden)] for k in range(2)]
            outs[which] = partial_output(lefts, weights, low)
            for k in range(group):
                source = outs.at[which, pl.ds(k * rows, rows)]
                target = pieces_out[g * group + k].at[pl.ds(which * rows, rows)]
                out_copies.append(stores.start(source, target))
    for copy in out_copies:
        copy.wait()


ANYWHERE = pl.BlockSpec(memory_space=pl.ANY)
IN_VMEM = pl.BlockSpec(memory_space=pltpu.VMEM)
IN_SMEM = pl.BlockSpec(memory_space=pltpu.SMEM)
SPARE = 16


def kernel_params(flops=10**11):
    return dict(
        compiler_params=pltpu.CompilerParams(vmem_limit_bytes=58 * 2**20),
        cost_estimate=pl.CostEstimate(flops=flops, bytes_accessed=flops // 10**3, transcendentals=0),
    )


def far_call(rows, first, pieces, weights):
    count, features = len(pieces), pieces[0].shape[1]
    hidden = weights[0][0].shape[0]
    height = count * rows
    bf = jnp.bfloat16
    shape = jax.ShapeDtypeStruct
    outs = pl.pallas_call(
        functools.partial(far_kernel, (count, rows)),
        out_shape=[shape((height, 2 * hidden), bf)] * 2
        + [shape((2 * rows + SPARE, features), bf)] * count,
        in_specs=[IN_SMEM] + [ANYWHERE] * (count + 8),
        out_specs=[ANYWHERE] * (2 + count),
        scratch_shapes=[pltpu.VMEM((height, features), bf)] * 2
        + [pltpu.VMEM((count, SPARE, 2 * rows), bf)]
        + [pltpu.VMEM((count, SPARE, features), bf)]
        + [pltpu.VMEM((height, 4 * hidden), bf)] * 2
        + [pltpu.VMEM((2 * hidden, features), bf)] * 4
        + [pltpu.VMEM((2, 2 * rows, features), bf)] * 2
        + [pltpu.SemaphoreType.DMA((3 * count + 8,)), pltpu.SemaphoreType.DMA((4 * count,))],
        **kernel_params(),
    )(first, *pieces, *sum(weights, ()))
    return outs[:2], outs[2:]


def sums_call(rows, first, near, far, near_over, far_over, far_values, weights):
    count, features = len(near), near[0].shape[1]
    hidden = weights[0][0].shape[0]
    height, tile = count * rows, 4 * rows
    bf, f32 = jnp.bfloat16, jnp.float32
    shape = jax.ShapeDtypeStruct
    outs = pl.pallas_call(
        functools.partial(sums_kernel, (count, rows)),
        out_shape=[shape((height, 2 * hidden), bf)] * 2
        + [shape((hidden, features), f32)] * 2
        + [shape((hidden, features), bf)] * 2
        + [shape((height, SPARE), f32)],
        in_specs=[IN_SMEM] + [ANYWHERE] * (3 * count + 7),
        out_specs=[ANYWHERE] * 6 + [IN_VMEM],
        scratch_shapes=[pltpu.VMEM((2, tile, features), bf)] * 2
        + [pltpu.VMEM((2, 4, SPARE, 2 * rows), bf)]
        + [pltpu.VMEM((2, tile, 2 * hidden), bf)] * 2
        + [pltpu.VMEM((4, hidden, features), f32)]
        + [pltpu.VMEM((2, hidden, features), bf)]
        + [pltpu.VMEM((2 * hidden, features), bf)] * 2
        + [pltpu.SemaphoreType.DMA((12 * count + 4,)), pltpu.SemaphoreType.DMA((count + 4,))],
        **kernel_params(),
    )(first, *near, *far, near_over, *far_over, *far_values, *sum(weights, ()))
    return outs[:2], outs[2:4], outs[4:6], outs[6]


def near_call(rows, first, score, near, values, weights):
    count, features = len(near), near[0].shape[1]
    hidden = weights[0][0].shape[0]
    tile = 4 * rows
    bf = jnp.bfloat16
    return pl.pallas_call(
        functools.partial(near_kernel, (count, rows)),
        out_shape=[jax.ShapeDtypeStruct((2 * rows + SPARE, features), bf)] * count,
        in_specs=[IN_SMEM, IN_VMEM] + [ANYWHERE] * (count + 10),
        out_specs=[ANYWHERE] * count,
        scratch_shapes=[pltpu.VMEM((2, tile, features), bf)] * 2
        + [pltpu.VMEM((2, 4, SPARE, 2 * rows), bf)]
        + [pltpu.VMEM((count, SPARE, features), bf)]
        + [pltpu.VMEM((2, tile, 2 * hidden), bf)] * 3
        + [pltpu.VMEM((2, tile, features), bf)]
        + [pltpu.VMEM((2 * hidden, features), bf)] * 4
        + [pltpu.SemaphoreType.DMA((4 * count + 8,)), pltpu.SemaphoreType.DMA((3 * count,))],
        **kernel_params(1000),
    )(first, score, *near, *values, *sum(weights, ()))


def coded(rows_of, features):
    high = lax.reduce_precision(rows_of, 8, 7)
    both = jnp.concatenate([high, rows_of - high], axis=1).astype(jnp.bfloat16)
    return jnp.pad(both, ((0, SPARE - both.shape[0]), (0, features - both.shape[1])))


class Grid:
    def __init__(self, n_exp, n_fsdp):
        self.nx, self.ny = n_exp // CORES, n_fsdp // DEPTH

    def move(self, array, to):
        pairs = []
        for x in range(self.nx):
            for c in range(CORES):
                for z in range(DEPTH):
                    for y in range(self.ny):
                        tx, tc, tz, ty = to(x, c, z, y)
                        pairs.append((self.index(x, c, z, y), self.index(tx, tc, tz, ty)))
        return lax.ppermute(array, AXES, pairs)

    def index(self, x, c, z, y):
        return ((x * CORES + c) * DEPTH + z) * self.ny + y

    def spread(self, array, dx, dy):
        if dx == dy == 0:
            return array
        return self.move(
            array, lambda x, c, z, y: ((x - dx) % self.nx, c, z, (y - dy) % self.ny)
        )

    def collect(self, array, dx, dy):
        if dx == dy == 0:
            return array
        return self.move(
            array, lambda x, c, z, y: ((x + dx) % self.nx, c, z, (y + dy) % self.ny)
        )

    def swap_core(self, array):
        return self.move(array, lambda x, c, z, y: (x, 1 - c, z, y))

    def swap_far(self, array):
        return self.move(array, lambda x, c, z, y: (x, c, z ^ 2, y))

    def swap_near(self, array):
        return self.move(array, lambda x, c, z, y: (x, c, z ^ 1, y))


def wide(array):
    return array.astype(jnp.float32)


def total(parts):
    out = wide(parts[0])
    for part in parts[1:]:
        out = out + wide(part)
    return out


def tie(*groups):
    return lax.optimization_barrier(groups)


def shards(tokens, expert_ids, gates, w_in, w_out, grad_y):
    rows, features = tokens.shape
    n_exp, n_fsdp = lax.axis_size("exp"), lax.axis_size("fsdp")
    grid = Grid(n_exp, n_fsdp)
    steps = [(xo, yo) for yo in range(grid.ny) for xo in range(grid.nx)]
    bf = jnp.bfloat16
    first = jnp.reshape(lax.axis_index("exp"), (1,))

    ids_row = expert_ids.T[None, :, :]
    named = ids_row == jnp.arange(n_exp, dtype=jnp.int32)[:, None, None]
    gate_rows = jnp.sum(jnp.where(named, gates.T[None], 0.0), axis=1)

    own = jnp.concatenate([tokens, grad_y, coded(gate_rows, features)], axis=0)
    own_pair = (w_in[0], w_out[0])
    near_pieces = [grid.spread(own, *step) for step in steps]
    far = grid.swap_far(own)
    far, near_pieces = tie(far, near_pieces)
    near_pair = tuple(grid.swap_near(part) for part in own_pair)
    far_pieces = [grid.spread(far, *step) for step in steps]
    near_over = grid.swap_core(jnp.concatenate(near_pieces, axis=0))
    other_own = tuple(grid.swap_core(part) for part in own_pair)
    other_near = tuple(grid.swap_core(part) for part in near_pair)
    weights = [own_pair, near_pair, other_own, other_near]
    far_values, far_out = far_call(rows, first, far_pieces, weights)

    far_home = [grid.collect(part, *step) for part, step in zip(far_out, steps)]
    far_over = [grid.swap_core(piece) for piece in far_pieces]
    near_values, keep, near_sums, score = sums_call(
        rows, first, near_pieces, far_pieces, near_over, far_over, far_values, weights[:2]
    )
    near_out = near_call(rows, first, score, near_pieces, near_values, weights)
    far_home, _ = tie(far_home, near_sums)
    near_sums = [grid.swap_near(part) for part in near_sums]
    last_out, near_sums[0] = tie(near_out[-1], near_sums[0])
    near_out = [*near_out[:-1], last_out]
    far_home = total(far_home)

    def score_of(home):
        return home[2 * rows :, :rows] + home[2 * rows :, rows : 2 * rows]

    far_home = jnp.concatenate(
        [far_home[: 2 * rows].astype(bf), coded(score_of(far_home), features)], axis=0
    )
    far_home = grid.swap_far(far_home)
    near_home = total([grid.collect(part, *step) for part, step in zip(near_out, steps)])

    home = near_home + wide(far_home)
    mixed, grad_tokens = home[:rows].astype(bf), home[rows : 2 * rows].astype(bf)
    score = score_of(home)[:n_exp]
    grad_gates = jnp.sum(jnp.where(named, score[:, None, :], 0.0), axis=0).T
    grad_in, grad_out = [mine + wide(theirs) for mine, theirs in zip(keep, near_sums)]
    return (mixed, grad_tokens, grad_in[None], grad_out[None], grad_gates)


def solution(mesh):
    rows = P(AXES, None)
    weights = P("exp", "fsdp", None)
    return jax.shard_map(
        shards,
        mesh=mesh,
        in_specs=(rows, rows, rows, weights, weights, rows),
        out_specs=(rows, rows, weights, weights, rows),
        check_vma=False,
    )
```

```python
import functools

import jax
import jax.numpy as jnp
from jax import lax
from jax.experimental import pallas as pl
from jax.experimental.pallas import tpu as pltpu
from jax.sharding import PartitionSpec as P

inv_sqrt_two = 0.7071067811865476
inv_sqrt_two_pi = 0.3989422804014327
AXES = ("exp", "fsdp")
CORES = 2
DEPTH = 4


def contract_first(left, right):
    return lax.dot_general(
        left, right, (((0,), (0,)), ((), ())), preferred_element_type=jnp.float32
    )


def contract_last(left, right):
    return lax.dot_general(
        left, right, (((1,), (1,)), ((), ())), preferred_element_type=jnp.float32
    )


def gelu_parts(values):
    cdf_part = 0.5 * (1.0 + lax.erf(values * inv_sqrt_two))
    return (
        values * cdf_part,
        cdf_part + values * jnp.exp(-0.5 * values * values) * inv_sqrt_two_pi,
    )


class Copies:
    def __init__(self, sems):
        self.sems, self.all = sems, []

    def start(self, source, target):
        copy = pltpu.make_async_copy(source, target, self.sems.at[len(self.all)])
        copy.start()
        self.all.append(copy)
        return copy

    def pair(self, sources, target):
        hidden = target.shape[0] // 2
        return Both(
            [self.start(sources[k], target.at[pl.ds(k * hidden, hidden)]) for k in range(2)]
        )


class Both:
    def __init__(self, copies):
        self.copies = copies

    def wait(self):
        for copy in self.copies:
            copy.wait()


def hidden_part(tok, grad, weight, scale, act_ref, hid_ref, columns):
    hidden = weight.shape[0] // 2
    pre = contract_last(tok, weight[:hidden, :])
    back = contract_last(grad, weight[hidden:, :])
    full, slope = gelu_parts(pre)
    act_ref[:, columns] = (full * scale).astype(jnp.bfloat16)
    hid_ref[:, columns] = (back * slope * scale).astype(jnp.bfloat16)
    return jnp.sum(full * back, axis=1, keepdims=True)


def gate_of(gate, expert):
    here = lax.broadcasted_iota(jnp.int32, gate.shape, 1) == expert
    return here, jnp.sum(jnp.where(here, gate, 0.0), axis=1, keepdims=True)


def decode(code, rows):
    wide_code = code.astype(jnp.float32)
    return (wide_code[:, :rows] + wide_code[:, rows:]).T


def far_kernel(plan, *refs):
    count, rows = plan
    refs = list(refs)
    take = lambda number: [refs.pop(0) for _ in range(number)]
    (first_ref,), pieces, weights_in = take(1), take(count), [take(2) for _ in range(4)]
    (act_out, hid_out), pieces_out = take(2), take(count)
    (tok, grad, coded_rows, extra), values = take(4), take(2)
    weights, stages, (sems_in, sems_out) = take(4), take(2), take(2)
    hidden = weights[0].shape[0] // 2
    tile = 2 * rows
    loads, stores = Copies(sems_in), Copies(sems_out)
    weight_ready, ready = [loads.pair(weights_in[0], weights[0])], []

    def load_tile(t):
        group = []
        for b in (2 * t, 2 * t + 1):
            at = pl.ds(b * rows, rows)
            group.append(loads.start(pieces[b].at[pl.ds(0, rows)], tok.at[at]))
            group.append(loads.start(pieces[b].at[pl.ds(rows, rows)], grad.at[at]))
            source = pieces[b].at[pl.ds(2 * rows, SPARE), pl.ds(0, 2 * rows)]
            group.append(loads.start(source, coded_rows.at[b]))
        ready.append(group)

    load_tile(0)
    for i in range(1, 4):
        weight_ready.append(loads.pair(weights_in[i], weights[i]))
    for t in range(1, count // 2):
        load_tile(t)
    first = first_ref[0]
    extra[...] = jnp.zeros_like(extra)
    staged, pending = [[], []], []
    for t in range(count // 2):
        span = pl.ds(t * tile, tile)
        for copy in ready[t]:
            copy.wait()
        gate = jnp.concatenate([decode(coded_rows[2 * t + k], rows) for k in range(2)], axis=0)
        total = 0.0
        for e in range(2):
            here, scale = gate_of(gate, first ^ e)
            part = 0.0
            if t == 0:
                weight_ready[2 * e].wait()
                weight_ready[2 * e + 1].wait()
            for i in (2 * e, 2 * e + 1):
                part = part + hidden_part(
                    tok[span, :],
                    grad[span, :],
                    weights[i],
                    scale,
                    values[0].at[span],
                    values[1].at[span],
                    slice(i * hidden, (i + 1) * hidden),
                )
            total = total + jnp.where(here, part, 0.0)
        for value, target in zip(values, (act_out, hid_out)):
            source = value.at[span, pl.ds(0, 2 * hidden)]
            pending.append(stores.start(source, target.at[span]))
        for k in range(2):
            b = 2 * t + k
            encode(total[k * rows : (k + 1) * rows, :], extra, b, rows)
            pending.append(stores.start(extra.at[b], pieces_out[b].at[pl.ds(2 * rows, SPARE)]))
        for copy in staged[t % 2]:
            copy.wait()
        staged[t % 2] = []
        for kind, (stage, low) in enumerate(zip(stages, (hidden, 0))):
            lefts = [values[kind].at[span, pl.ds(i * hidden, hidden)] for i in range(4)]
            stage[t % 2] = partial_output(lefts, weights, low)
            for k in range(2):
                source = stage.at[t % 2, pl.ds(k * rows, rows)]
                target = pieces_out[2 * t + k].at[pl.ds(kind * rows, rows)]
                staged[t % 2].append(stores.start(source, target))
    for copy in pending + staged[0] + staged[1]:
        copy.wait()


def encode(score, extra, b, rows):
    rest = score.T
    high = rest.astype(jnp.bfloat16)
    extra[b, :, pl.ds(0, rows)] = high
    extra[b, :, pl.ds(rows, rows)] = (rest - high.astype(jnp.float32)).astype(jnp.bfloat16)


def partial_output(lefts, weights, low):
    hidden = weights[0].shape[0] // 2
    out = 0.0
    for left, weight in zip(lefts, weights):
        out = out + jnp.dot(
            left[...], weight[low : low + hidden, :], preferred_element_type=jnp.float32
        )
    return out.astype(jnp.bfloat16)


def split(stack, count, rows):
    step = 2 * rows + SPARE
    return [stack.at[pl.ds(b * step, step)] for b in range(count)]


def load_blocks(loads, blocks, slot, tok, grad, coded_rows, rows):
    started = []
    for k, block in enumerate(blocks):
        at = pl.ds(k * rows, rows)
        started.append(loads.start(block.at[pl.ds(0, rows)], tok.at[slot, at]))
        started.append(loads.start(block.at[pl.ds(rows, rows)], grad.at[slot, at]))
        if coded_rows is not None:
            source = block.at[pl.ds(2 * rows, SPARE), pl.ds(0, 2 * rows)]
            started.append(loads.start(source, coded_rows.at[slot, k]))
    return started


def add_sums(totals, acts, hids, tok, grad, slot, empty, results=None):
    hidden = totals.shape[1]
    for which, (left, right) in enumerate(((hids, tok), (acts, grad))):
        for k in range(2):
            out = contract_first(left[slot, :, k * hidden : (k + 1) * hidden], right[slot])
            if not empty:
                out = out + totals[2 * which + k]
            if results is None or k == 0:
                totals[2 * which + k] = out
            else:
                results[which] = out.astype(jnp.bfloat16)


def sums_kernel(plan, *refs):
    count, rows = plan
    refs = list(refs)
    take = lambda number: [refs.pop(0) for _ in range(number)]
    (first_ref,), near, far, (near_over,) = take(1), take(count), take(count), take(1)
    far_over, far_values = take(count), take(2)
    weights_in, near_values = [take(2) for _ in range(2)], take(2)
    keep_out, near_sums, (score,) = take(2), take(2), take(1)
    tok, grad, coded_rows, acts, hids, totals, results = take(7)
    weights, (sems_in, sems_out) = take(2), take(2)
    group = 4
    tile = group * rows
    hidden = weights[0].shape[0] // 2
    loads, stores = Copies(sems_in), Copies(sems_out)
    lists = [near, far, split(near_over, count, rows), far_over]
    steps = [
        (kind, g, blocks[g * group : (g + 1) * group])
        for kind, blocks in enumerate(lists)
        for g in range(count // group)
    ]

    def load(n):
        kind, g, blocks = steps[n]
        codes = None if kind == 1 else coded_rows
        started = load_blocks(loads, blocks, n % 2, tok, grad, codes, rows)
        if kind == 1:
            for source, target in zip(far_values, (acts, hids)):
                source = source.at[pl.ds(g * tile, tile)]
                started.append(loads.start(source, target.at[n % 2]))
        return started

    weight_ready = [loads.pair(weights_in[0], weights[0])]
    ready = load(0)
    weight_ready.append(loads.pair(weights_in[1], weights[1]))
    first = first_ref[0]
    saved = [[], []]
    for n, (kind, g, blocks) in enumerate(steps):
        slot = n % 2
        for copy in saved[1 - slot]:
            copy.wait()
        saved[1 - slot] = []
        coming = load(n + 1) if n + 1 < len(steps) else []
        for copy in ready:
            copy.wait()
        ready = coming
        if kind != 1:
            gate = jnp.concatenate([decode(coded_rows[slot, k], rows) for k in range(group)], axis=0)
            here, scale = gate_of(gate, first)
            part = 0.0
            if n == 0:
                weight_ready[0].wait()
                weight_ready[1].wait()
            for k in range(2):
                columns = slice(k * hidden, (k + 1) * hidden)
                part = part + hidden_part(
                    tok[slot], grad[slot], weights[k], scale, acts.at[slot], hids.at[slot], columns
                )
        if kind == 0:
            span = pl.ds(g * tile, tile)
            score[span, :] = jnp.where(here, part, 0.0)
            saved[slot] = [
                stores.start(acts.at[slot], near_values[0].at[span]),
                stores.start(hids.at[slot], near_values[1].at[span]),
            ]
        last = n + 1 == len(steps)
        add_sums(totals, acts, hids, tok, grad, slot, n == 0, results if last else None)
    tail = [stores.start(totals.at[2 * which], keep_out[which]) for which in range(2)]
    tail += [stores.start(results.at[which], near_sums[which]) for which in range(2)]
    for copy in saved[0] + saved[1] + tail:
        copy.wait()


def near_kernel(plan, *refs):
    count, rows = plan
    refs = list(refs)
    take = lambda number: [refs.pop(0) for _ in range(number)]
    (first_ref, score), near, values_in = take(2), take(count), take(2)
    weights_in = [take(2) for _ in range(4)]
    pieces_out = take(count)
    tok, grad, coded_rows, extra, acts, hids, others, outs = take(8)
    weights, (sems_in, sems_out) = take(4), take(2)
    hidden = weights[0].shape[0] // 2
    group = 4
    tile = group * rows
    loads, stores = Copies(sems_in), Copies(sems_out)

    def load(g):
        blocks, span = near[g * group : (g + 1) * group], pl.ds(g * tile, tile)
        started = load_blocks(loads, blocks, g % 2, tok, grad, coded_rows, rows)
        for source, target in zip(values_in, (acts, hids)):
            started.append(loads.start(source.at[span], target.at[g % 2]))
        return started

    weight_ready = {2: loads.pair(weights_in[2], weights[2])}
    ready = load(0)
    for i in (3, 0, 1):
        weight_ready[i] = loads.pair(weights_in[i], weights[i])
    first = first_ref[0]
    extra[...] = jnp.zeros_like(extra)
    out_copies = []
    for g in range(count // group):
        slot = g % 2
        coming = load(g + 1) if (g + 1) * group < count else []
        for copy in ready + out_copies:
            copy.wait()
        ready, out_copies = coming, []
        gate = jnp.concatenate([decode(coded_rows[slot, k], rows) for k in range(group)], axis=0)
        here, scale = gate_of(gate, first ^ 1)
        part = 0.0
        for k in range(2):
            if g == 0:
                weight_ready[2 + k].wait()
            columns = slice(k * hidden, (k + 1) * hidden)
            part = part + hidden_part(
                tok[slot], grad[slot], weights[2 + k], scale, others.at[0], others.at[1], columns
            )
        total = score[pl.ds(g * tile, tile), :] + jnp.where(here, part, 0.0)
        if g == 0:
            weight_ready[0].wait()
            weight_ready[1].wait()
        for k in range(group):
            b = g * group + k
            encode(total[k * rows : (k + 1) * rows, :], extra, b, rows)
            out_copies.append(stores.start(extra.at[b], pieces_out[b].at[pl.ds(2 * rows, SPARE)]))
        for which, (mine, low) in enumerate(((acts, hidden), (hids, 0))):
            lefts = [mine.at[slot, :, pl.ds(k * hidden, hidden)] for k in range(2)]
            lefts += [others.at[which, :, pl.ds(k * hidden, hidden)] for k in range(2)]
            outs[which] = partial_output(lefts, weights, low)
            for k in range(group):
                source = outs.at[which, pl.ds(k * rows, rows)]
                target = pieces_out[g * group + k].at[pl.ds(which * rows, rows)]
                out_copies.append(stores.start(source, target))
    for copy in out_copies:
        copy.wait()


ANYWHERE = pl.BlockSpec(memory_space=pl.ANY)
IN_VMEM = pl.BlockSpec(memory_space=pltpu.VMEM)
IN_SMEM = pl.BlockSpec(memory_space=pltpu.SMEM)
SPARE = 16


def kernel_params(flops=10**11):
    return dict(
        compiler_params=pltpu.CompilerParams(vmem_limit_bytes=58 * 2**20),
        cost_estimate=pl.CostEstimate(flops=flops, bytes_accessed=flops // 10**3, transcendentals=0),
    )


def far_call(rows, first, pieces, weights):
    count, features = len(pieces), pieces[0].shape[1]
    hidden = weights[0][0].shape[0]
    height = count * rows
    bf = jnp.bfloat16
    shape = jax.ShapeDtypeStruct
    outs = pl.pallas_call(
        functools.partial(far_kernel, (count, rows)),
        out_shape=[shape((height, 2 * hidden), bf)] * 2
        + [shape((2 * rows + SPARE, features), bf)] * count,
        in_specs=[IN_SMEM] + [ANYWHERE] * (count + 8),
        out_specs=[ANYWHERE] * (2 + count),
        scratch_shapes=[pltpu.VMEM((height, features), bf)] * 2
        + [pltpu.VMEM((count, SPARE, 2 * rows), bf)]
        + [pltpu.VMEM((count, SPARE, features), bf)]
        + [pltpu.VMEM((height, 4 * hidden), bf)] * 2
        + [pltpu.VMEM((2 * hidden, features), bf)] * 4
        + [pltpu.VMEM((2, 2 * rows, features), bf)] * 2
        + [pltpu.SemaphoreType.DMA((3 * count + 8,)), pltpu.SemaphoreType.DMA((4 * count,))],
        **kernel_params(),
    )(first, *pieces, *sum(weights, ()))
    return outs[:2], outs[2:]


def sums_call(rows, first, near, far, near_over, far_over, far_values, weights):
    count, features = len(near), near[0].shape[1]
    hidden = weights[0][0].shape[0]
    height, tile = count * rows, 4 * rows
    bf, f32 = jnp.bfloat16, jnp.float32
    shape = jax.ShapeDtypeStruct
    outs = pl.pallas_call(
        functools.partial(sums_kernel, (count, rows)),
        out_shape=[shape((height, 2 * hidden), bf)] * 2
        + [shape((hidden, features), f32)] * 2
        + [shape((hidden, features), bf)] * 2
        + [shape((height, SPARE), f32)],
        in_specs=[IN_SMEM] + [ANYWHERE] * (3 * count + 7),
        out_specs=[ANYWHERE] * 6 + [IN_VMEM],
        scratch_shapes=[pltpu.VMEM((2, tile, features), bf)] * 2
        + [pltpu.VMEM((2, 4, SPARE, 2 * rows), bf)]
        + [pltpu.VMEM((2, tile, 2 * hidden), bf)] * 2
        + [pltpu.VMEM((4, hidden, features), f32)]
        + [pltpu.VMEM((2, hidden, features), bf)]
        + [pltpu.VMEM((2 * hidden, features), bf)] * 2
        + [pltpu.SemaphoreType.DMA((12 * count + 4,)), pltpu.SemaphoreType.DMA((count + 4,))],
        **kernel_params(),
    )(first, *near, *far, near_over, *far_over, *far_values, *sum(weights, ()))
    return outs[:2], outs[2:4], outs[4:6], outs[6]


def near_call(rows, first, score, near, values, weights):
    count, features = len(near), near[0].shape[1]
    hidden = weights[0][0].shape[0]
    tile = 4 * rows
    bf = jnp.bfloat16
    return pl.pallas_call(
        functools.partial(near_kernel, (count, rows)),
        out_shape=[jax.ShapeDtypeStruct((2 * rows + SPARE, features), bf)] * count,
        in_specs=[IN_SMEM, IN_VMEM] + [ANYWHERE] * (count + 10),
        out_specs=[ANYWHERE] * count,
        scratch_shapes=[pltpu.VMEM((2, tile, features), bf)] * 2
        + [pltpu.VMEM((2, 4, SPARE, 2 * rows), bf)]
        + [pltpu.VMEM((count, SPARE, features), bf)]
        + [pltpu.VMEM((2, tile, 2 * hidden), bf)] * 3
        + [pltpu.VMEM((2, tile, features), bf)]
        + [pltpu.VMEM((2 * hidden, features), bf)] * 4
        + [pltpu.SemaphoreType.DMA((4 * count + 8,)), pltpu.SemaphoreType.DMA((3 * count,))],
        **kernel_params(1000),
    )(first, score, *near, *values, *sum(weights, ()))


def coded(rows_of, features):
    high = lax.reduce_precision(rows_of, 8, 7)
    both = jnp.concatenate([high, rows_of - high], axis=1).astype(jnp.bfloat16)
    return jnp.pad(both, ((0, SPARE - both.shape[0]), (0, features - both.shape[1])))


class Grid:
    def __init__(self, n_exp, n_fsdp):
        self.nx, self.ny = n_exp // CORES, n_fsdp // DEPTH

    def move(self, array, to):
        pairs = []
        for x in range(self.nx):
            for c in range(CORES):
                for z in range(DEPTH):
                    for y in range(self.ny):
                        tx, tc, tz, ty = to(x, c, z, y)
                        pairs.append((self.index(x, c, z, y), self.index(tx, tc, tz, ty)))
        return lax.ppermute(array, AXES, pairs)

    def index(self, x, c, z, y):
        return ((x * CORES + c) * DEPTH + z) * self.ny + y

    def spread(self, array, dx, dy):
        if dx == dy == 0:
            return array
        return self.move(
            array, lambda x, c, z, y: ((x - dx) % self.nx, c, z, (y - dy) % self.ny)
        )

    def collect(self, array, dx, dy):
        if dx == dy == 0:
            return array
        return self.move(
            array, lambda x, c, z, y: ((x + dx) % self.nx, c, z, (y + dy) % self.ny)
        )

    def swap_core(self, array):
        return self.move(array, lambda x, c, z, y: (x, 1 - c, z, y))

    def swap_far(self, array):
        return self.move(array, lambda x, c, z, y: (x, c, z ^ 2, y))

    def swap_near(self, array):
        return self.move(array, lambda x, c, z, y: (x, c, z ^ 1, y))


def wide(array):
    return array.astype(jnp.float32)


def total(parts):
    out = wide(parts[0])
    for part in parts[1:]:
        out = out + wide(part)
    return out


def tie(*groups):
    return lax.optimization_barrier(groups)


def shards(tokens, expert_ids, gates, w_in, w_out, grad_y):
    rows, features = tokens.shape
    n_exp, n_fsdp = lax.axis_size("exp"), lax.axis_size("fsdp")
    grid = Grid(n_exp, n_fsdp)
    steps = [(xo, yo) for yo in range(grid.ny) for xo in range(grid.nx)]
    bf = jnp.bfloat16
    first = jnp.reshape(lax.axis_index("exp"), (1,))

    ids_row = expert_ids.T[None, :, :]
    named = ids_row == jnp.arange(n_exp, dtype=jnp.int32)[:, None, None]
    gate_rows = jnp.sum(jnp.where(named, gates.T[None], 0.0), axis=1)

    own = jnp.concatenate([tokens, grad_y, coded(gate_rows, features)], axis=0)
    own_pair = (w_in[0], w_out[0])
    near_pieces = [grid.spread(own, *step) for step in steps]
    far = grid.swap_far(own)
    far, near_pieces = tie(far, near_pieces)
    near_pair = tuple(grid.swap_near(part) for part in own_pair)
    far_pieces = [grid.spread(far, *step) for step in steps]
    near_over = grid.swap_core(jnp.concatenate(near_pieces, axis=0))
    other_own = tuple(grid.swap_core(part) for part in own_pair)
    other_near = tuple(grid.swap_core(part) for part in near_pair)
    weights = [own_pair, near_pair, other_own, other_near]
    far_values, far_out = far_call(rows, first, far_pieces, weights)

    far_home = [grid.collect(part, *step) for part, step in zip(far_out, steps)]
    far_over = [grid.swap_core(piece) for piece in far_pieces]
    near_values, keep, near_sums, score = sums_call(
        rows, first, near_pieces, far_pieces, near_over, far_over, far_values, weights[:2]
    )
    near_out = near_call(rows, first, score, near_pieces, near_values, weights)
    far_home, _ = tie(far_home, near_sums)
    near_sums = [grid.swap_near(part) for part in near_sums]
    last_out, near_sums[0] = tie(near_out[-1], near_sums[0])
    near_out = [*near_out[:-1], last_out]
    far_home = total(far_home)

    def score_of(home):
        return home[2 * rows :, :rows] + home[2 * rows :, rows : 2 * rows]

    far_home = jnp.concatenate(
        [far_home[: 2 * rows].astype(bf), coded(score_of(far_home), features)], axis=0
    )
    far_home = grid.swap_far(far_home)
    near_home = total([grid.collect(part, *step) for part, step in zip(near_out, steps)])

    home = near_home + wide(far_home)
    mixed, grad_tokens = home[:rows].astype(bf), home[rows : 2 * rows].astype(bf)
    score = score_of(home)[:n_exp]
    grad_gates = jnp.sum(jnp.where(named, score[:, None, :], 0.0), axis=0).T
    grad_in, grad_out = [mine + wide(theirs) for mine, theirs in zip(keep, near_sums)]
    return (mixed, grad_tokens, grad_in[None], grad_out[None], grad_gates)


def solution(mesh):
    rows = P(AXES, None)
    weights = P("exp", "fsdp", None)
    return jax.shard_map(
        shards,
        mesh=mesh,
        in_specs=(rows, rows, rows, weights, weights, rows),
        out_specs=(rows, rows, weights, weights, rows),
        check_vma=False,
    )
```
